256 devices in a mesh: samp: 64 (over x, y, z_lo), strip: 4 (over z_hi, core).
Axes of the slice: x: 4, y: 4, z: 8 (z_hi: 2, z_lo: 4; z = z_hi * 4 + z_lo), core: 2. Of those that a mesh axis runs over, the one named last changes fastest.
Arguments:
- initial_state: float32 [256, 4096], P('strip'), may hold values from -6 to 6
- target: float32 [256, 4096], P('strip'), may hold values from -6 to 6
- control: float32 [256, 4096], P('strip'), may hold values from -6 to 6
- point_index: int32 [64], P('samp'), may hold values from 0 to 65535
- generator: int32 [32, 32], replicated, may hold values from 1 to 65535
Outputs:
- new_control: float32 [256, 4096], P('strip')
- final_state: float32 [64, 256, 4096], P('samp', 'strip')
The draws below stay inside these ranges and needn't reach their ends.
All inputs are finite; a program needn't handle non-finite values.
Results may differ from the reference program's by a relative error of at most 0.0003.
Values sent between devices are 32-bit elements; how exact they have to be, the bound alone decides.
No kernel may reach another device: no remote copies, remote signals or barrier semaphores. Data moves between devices by JAX's collectives and lax.ppermute only.
A program may use at most 64 MiB of HBM per device.

```python
import jax
import jax.numpy as jnp
from jax import lax

NY = 4096
MODES = 32
STEPS = 3
SAMPLES = 64
NX = 256


def place_ends(array, key, smallest, largest):
    longest = array.shape.index(max(array.shape))
    spots = []
    for shift in (0, 1):
        where = [jax.random.randint(jax.random.fold_in(key, axis), (), 0, length) for axis, length in enumerate(array.shape)]
        where[longest] = (where[longest] + shift) % array.shape[longest]
        spots.append(tuple(where))
    return array.at[spots[0]].set(smallest).at[spots[1]].set(largest)


def shard_levels(key, dims, split, smallest, top_value):
    loudness, own = 1.0, jax.random.fold_in(key, 6)
    for position, shards_of in split:
        steps = jnp.exp(jax.random.uniform(jax.random.fold_in(own, position), (shards_of,), jnp.float32, smallest / len(split), top_value / len(split)))
        loudness = loudness * jnp.repeat(steps, dims[position] // shards_of).reshape([-1 if axis == position else 1 for axis in range(len(dims))])
    return loudness


def noise(own_key, extent, spread, bound, pieces=(), kind=jnp.bfloat16):
    gain = shard_levels(own_key, extent, pieces, -0.22, 0.18) if pieces else 1.0
    drawn = jax.random.normal(own_key, extent, jnp.float32) * spread * gain
    return jnp.minimum(jnp.maximum(drawn, -bound), bound).astype(kind)


def setup_inputs(seed: int = 0) -> dict:
    key_list = jax.random.split(jax.random.key(seed), 6)
    return {
        "initial_state": noise(key_list[0], (NX, NY), 1.0, 6.0, ((0, 4),), jnp.float32),
        "target": noise(key_list[1], (NX, NY), 1.0, 6.0, ((0, 4),), jnp.float32),
        "control": noise(key_list[2], (NX, NY), 1.0, 6.0, ((0, 4),), jnp.float32),
        "point_index": place_ends(jax.random.randint(key_list[3], (SAMPLES,), 0, 65536), jax.random.fold_in(key_list[3], 1), 0, 65535).astype(jnp.int32),
        "generator": place_ends(jax.random.randint(key_list[4], (MODES, MODES), 1, 65536), jax.random.fold_in(key_list[4], 1), 1, 65535).astype(jnp.int32),
    }


TWO_PI = 6.283185307179586
DT = 0.12
REG = 0.1
RATE = 1.0

def mode_weights(modes):
    ranks = jnp.arange(1, modes + 1, dtype=jnp.float32)
    harmonic = jnp.sum(1.0 / ranks)
    return 4.0 / harmonic / jnp.sqrt(ranks[:, None] * ranks[None, :])

def sine_table(places, modes, period):
    freq = jnp.arange(1, modes + 1, dtype=jnp.int32)
    turns = freq[:, None] * places[None, :] % period
    return jnp.sin(TWO_PI * turns.astype(jnp.float32) / period)

def diffuse(coef, field):
    middle = field[..., 1:-1, :]
    center = coef[..., 1:-1, :]
    total = 0.5 * (center + coef[..., :-2, :]) * (field[..., :-2, :] - middle)
    total = total + 0.5 * (center + coef[..., 2:, :]) * (field[..., 2:, :] - middle)
    total = total + 0.5 * (center + jnp.roll(center, 1, -1)) * (jnp.roll(middle, 1, -1) - middle)
    total = total + 0.5 * (center + jnp.roll(center, -1, -1)) * (jnp.roll(middle, -1, -1) - middle)
    return total

def wrapped(field):
    return jnp.concatenate([field[-1:], field, field[:1]], axis=0)

def reference(initial_state, target, control, point_index, generator):
    weights = mode_weights(MODES)
    row_table = sine_table(jnp.arange(NX, dtype=jnp.int32), MODES, NX)
    col_table = sine_table(jnp.arange(NY, dtype=jnp.int32), MODES, NY)

    def one(total, index):
        cells = index * generator % 65536
        coeff = (cells.astype(jnp.float32) / 65536.0 - 0.5) * weights
        inner = jnp.dot(coeff, col_table, precision=lax.Precision.HIGHEST, preferred_element_type=jnp.float32)
        field_log = jnp.dot(row_table.T, inner, precision=lax.Precision.HIGHEST, preferred_element_type=jnp.float32)
        coef = 1.0 + 0.8 * jnp.tanh(field_log)
        coef_ext = wrapped(coef)
        state = initial_state
        for step in range(STEPS):
            state = state + DT * (diffuse(coef_ext, wrapped(state)) + control)
        costate = state - target
        summed = costate
        for step in range(STEPS - 1):
            costate = costate + DT * diffuse(coef_ext, wrapped(costate))
            summed = summed + costate
        return (total + DT * summed, state)
    start = jnp.zeros((NX, NY), jnp.float32)
    total, finals = lax.scan(one, start, point_index)
    grad = total / SAMPLES + REG * control
    return (control - RATE * grad, finals)
```

```python
import jax
import jax.numpy as jnp
import numpy as np
from jax import lax
from jax.sharding import PartitionSpec as P

STEPS = 3
TWO_PI = 6.283185307179586
DT = 0.12
REG = 0.1
RATE = 1.0
HALO = 2 * STEPS - 1

SAMP = np.arange(64).reshape(4, 4, 4)
ALONG_Z = SAMP.reshape(16, 4).tolist()
ALONG_XY = SAMP.transpose(2, 0, 1).reshape(4, 16).tolist()


def mode_weights(modes):
    ranks = jnp.arange(1, modes + 1, dtype=jnp.float32)
    harmonic = jnp.sum(1.0 / ranks)
    return 4.0 / harmonic / jnp.sqrt(ranks[:, None] * ranks[None, :])


def sine_table(places, modes, period):
    freq = jnp.arange(1, modes + 1, dtype=jnp.int32)
    turns = freq[:, None] * places[None, :] % period
    return jnp.sin(TWO_PI * turns.astype(jnp.float32) / period)


def diffuse(coef, field):
    middle = field[1:-1]
    center = coef[1:-1]
    total = 0.5 * (center + coef[:-2]) * (field[:-2] - middle)
    total = total + 0.5 * (center + coef[2:]) * (field[2:] - middle)
    total = total + 0.5 * (center + jnp.roll(center, 1, -1)) * (jnp.roll(middle, 1, -1) - middle)
    total = total + 0.5 * (center + jnp.roll(center, -1, -1)) * (jnp.roll(middle, -1, -1) - middle)
    return total


def strip_shift(step):
    pairs = []
    for samp in range(64):
        for strip in range(4):
            to = (strip + step) % 4
            other = samp if to // 2 == strip // 2 else samp ^ 2
            pairs.append((samp * 4 + strip, other * 4 + to))
    return pairs


def on_device(initial_state, target, control, point_index, generator):
    rows, width = initial_state.shape
    modes = generator.shape[0]
    grid_rows = rows * lax.axis_size("strip")
    count = lax.axis_size("samp")
    h = HALO
    tail = jnp.concatenate([initial_state[-h:], control[-(h - 1):], target[-2:]], axis=0)
    head = jnp.concatenate([initial_state[:h], control[: h - 1], target[:2]], axis=0)
    before = lax.ppermute(tail, ("samp", "strip"), strip_shift(1))
    after = lax.ppermute(head, ("samp", "strip"), strip_shift(-1))

    first_row = lax.axis_index("strip") * rows
    cells = point_index[:, None] * generator % 65536
    coeff = (cells.astype(jnp.float32) / 65536.0 - 0.5) * mode_weights(modes)
    col_table = sine_table(jnp.arange(width, dtype=jnp.int32), modes, width)
    inner = jnp.dot(coeff, col_table, precision=lax.Precision.HIGHEST)
    places = (first_row - h + jnp.arange(rows + 2 * h, dtype=jnp.int32)) % grid_rows
    table = sine_table(places, modes, grid_rows)
    field_log = jnp.dot(table.T, inner, precision=lax.Precision.HIGHEST)
    coef = 1.0 + 0.8 * jnp.tanh(field_log)

    state = jnp.concatenate([before[:h], initial_state, after[:h]], axis=0)
    source = jnp.concatenate([before[h : 2 * h - 1], control, after[h : 2 * h - 1]], axis=0)
    wanted = jnp.concatenate([before[2 * h - 1 :], target, after[2 * h - 1 :]], axis=0)
    for step in range(STEPS):
        state = state[1:-1] + DT * (diffuse(coef, state) + source)
        coef, source = coef[1:-1], source[1:-1]
    lam = state - wanted
    state = state[2:-2]
    summed = lam[2:-2]
    for step in range(STEPS - 1):
        lam = lam[1:-1] + DT * diffuse(coef, lam)
        coef = coef[1:-1]
        trim = STEPS - 2 - step
        summed = summed + lam[trim : lam.shape[0] - trim]
    partial = DT * summed
    blocks = partial.reshape(8, 8, 8, 512).transpose(0, 2, 1, 3).reshape(16, 4, 8, 512)
    blocks = jnp.sum(lax.all_to_all(blocks, "samp", 0, 0, axis_index_groups=ALONG_XY, tiled=True), axis=0)
    blocks = jnp.sum(lax.all_to_all(blocks, "samp", 0, 0, axis_index_groups=ALONG_Z, tiled=True), axis=0)
    blocks = jnp.broadcast_to(blocks[None], (4, 8, 512))
    blocks = lax.all_to_all(blocks, "samp", 0, 0, axis_index_groups=ALONG_Z, tiled=True)
    blocks = jnp.broadcast_to(blocks[None], (16, 4, 8, 512))
    blocks = lax.all_to_all(blocks, "samp", 0, 0, axis_index_groups=ALONG_XY, tiled=True)
    total = blocks.reshape(8, 8, 8, 512).transpose(0, 2, 1, 3).reshape(rows, width)
    new_control = control - RATE * (total / count + REG * control)
    return (new_control, state[None])


def solution(mesh):
    placed = (P("strip", None), P("strip", None), P("strip", None), P("samp"), P())
    return jax.shard_map(
        on_device,
        mesh=mesh,
        in_specs=placed,
        out_specs=(P("strip", None), P("samp", "strip", None)),
        check_vma=False,
    )
```

```python
import jax
import jax.numpy as jnp
import numpy as np
from jax import lax
from jax.experimental import pallas as pl
from jax.experimental.pallas import tpu as pltpu
from jax.sharding import PartitionSpec as P

STEPS = 3
TWO_PI = 6.283185307179586
DT = 0.12
REG = 0.1
RATE = 1.0
SAMPLES = 64
MODES = 32
HALO = 2 * STEPS - 1
TILE = 64
HALF = TILE // 2
COLS = HALF + 2 * HALO
TALL = TILE + 16

SAMP = np.arange(64).reshape(4, 4, 4)
ALONG_Z = SAMP.reshape(16, 4).tolist()
ALONG_XY = SAMP.transpose(2, 0, 1).reshape(4, 16).tolist()


def mode_scale(modes):
    ranks = jnp.arange(1, modes + 1, dtype=jnp.float32)
    return 4.0 / jnp.sum(1.0 / ranks), 1.0 / jnp.sqrt(ranks)


def sine_table(places, modes, period):
    freq = jnp.arange(1, modes + 1, dtype=jnp.int32)
    turns = freq[:, None] * places[None, :] % period
    return jnp.sin(TWO_PI * turns.astype(jnp.float32) / period)


def split(value):
    high = value.astype(jnp.bfloat16)
    return high, (value - high.astype(jnp.float32)).astype(jnp.bfloat16)


def window_kernel(where_ref, *refs):
    ins, out = refs[:9], refs[9]
    odd = where_ref[3]
    for f in range(3):
        row = jnp.concatenate([r[...] for r in ins[3 * f : 3 * f + 3]], axis=1)
        even_part = row[:, 128 - HALO : 256 - HALO]
        odd_part = row[:, 192 - HALO : 320 - HALO]
        out[f] = jnp.where(odd == 1, odd_part, even_part)


def own_windows(fields, tile):
    rows, width = fields[0].shape
    blocks = width // 128
    middle = tile // 2
    where = jnp.stack([(middle - 1) % blocks, middle, (middle + 1) % blocks, tile % 2]).astype(jnp.int32)
    specs = [pl.BlockSpec((rows, 128), lambda i, w, n=n: (0, w[n])) for n in range(3)]
    return pl.pallas_call(
        window_kernel,
        out_shape=jax.ShapeDtypeStruct((3, rows, 128), jnp.float32),
        grid_spec=pltpu.PrefetchScalarGridSpec(
            num_scalar_prefetch=1,
            grid=(1,),
            in_specs=specs * 3,
            out_specs=pl.BlockSpec((3, rows, 128), lambda i, w: (0, 0, 0)),
        ),
        name="own_windows",
    )(where, *[f for f in fields for _ in range(3)])


def tile_kernel(points_ref, gen_ref, col_ref, row_ref, x_ref, out_ref, inner_ref, kx_ref, ky_ref, v_ref, g_ref, t_ref, s_ref):
    f32 = jnp.float32
    lane = lax.broadcasted_iota(jnp.int32, (1, 128), 1)
    left = lane < SAMPLES

    for f, ref, scale in ((0, v_ref, 1.0), (1, g_ref, DT), (2, t_ref, 1.0)):
        x = x_ref[f] * scale
        for j in range(COLS):
            ref[j] = jnp.where(left, x[:, j : j + 1], x[:, j + HALF : j + HALF + 1])

    points = points_ref[...]
    for p in range(MODES):
        cells = (points * gen_ref[:, p : p + 1]) & 65535
        coords = cells.astype(f32) * (1.0 / 65536.0) - 0.5
        both = jnp.concatenate([jnp.where(left, coords, 0.0), jnp.where(left, 0.0, coords)], axis=0)
        high, low = split(both)
        inner_ref[48 * p : 48 * p + 48, :] = jnp.dot(
            col_ref[...], jnp.concatenate([high, low, high], axis=0), preferred_element_type=f32
        )

    def fields(j, before):
        high, low = split(inner_ref[pl.ds(j, MODES, stride=48), :])
        log = jnp.dot(row_ref[...], jnp.concatenate([high, low, high], axis=0), preferred_element_type=f32)
        k = 0.5 * DT + (0.5 * DT * 0.8) * jnp.tanh(log)
        kx_ref[j] = before + k
        ky_ref[j] = k + pltpu.roll(k, TALL - 1, 0)
        return k

    lax.fori_loop(0, COLS, fields, jnp.zeros((TALL, 128), f32))

    def divergence(j, carry):
        v, left_flux = carry
        right = v_ref[j + 1]
        right_flux = kx_ref[j + 1] * (right - v)
        down_flux = ky_ref[j] * (pltpu.roll(v, TALL - 1, 0) - v)
        new = v + ((right_flux - left_flux) + (down_flux - pltpu.roll(down_flux, 1, 0)))
        return new, (right, right_flux)

    def sweep(first, body):
        v = v_ref[first]
        start = (v, kx_ref[first] * (v - v_ref[first - 1]))
        return start, first, COLS - first

    def state_step(j, carry):
        new, after = divergence(j, carry)
        v_ref[j] = new + g_ref[j]
        return after

    def last_state_step(j, carry):
        new, after = divergence(j, carry)
        v_ref[j] = new + g_ref[j] - t_ref[j]
        return after

    def first_costate_step(j, carry):
        new, after = divergence(j, carry)
        s_ref[j] = carry[0] + new
        v_ref[j] = new
        return after

    for t, body in enumerate((state_step, state_step, last_state_step, first_costate_step)):
        start, low_j, high_j = sweep(t + 1, body)
        lax.fori_loop(low_j, high_j, body, start)

    source = lax.broadcasted_iota(jnp.int32, (256, 128), 0) % 128 // SAMPLES
    place = lax.broadcasted_iota(jnp.int32, (256, 128), 1) // HALF % 2
    add_samples = (source == place).astype(f32).astype(jnp.bfloat16)

    def last_costate_step(j, carry):
        total, carry = carry
        new, after = divergence(j, carry)
        high, low = split((s_ref[j] + new)[8 : 8 + TILE])
        sums = jnp.dot(jnp.concatenate([high, low], axis=1), add_samples, preferred_element_type=f32)
        return jnp.where(lane % HALF == j - HALO, sums, total), after

    start, low_j, high_j = sweep(HALO, last_costate_step)
    total, _ = lax.fori_loop(low_j, high_j, last_costate_step, (jnp.zeros((TILE, 128), f32), start))

    total = jnp.where(left, total[:HALF], total[HALF:])
    control = x_ref[1]
    top = pltpu.roll(control[8 : 8 + HALF], 128 - HALO, 1)
    bottom = pltpu.roll(control[8 + HALF : 8 + TILE], TILE - HALO, 1)
    control = jnp.where(left, top, bottom)
    out_ref[...] = control - RATE * (total * (DT / SAMPLES) + REG * control)


def tile_gradient(points, gen_t, col_parts, row_parts, x):
    big = pltpu.VMEM((COLS, TALL, 128), jnp.float32)
    return pl.pallas_call(
        tile_kernel,
        out_shape=jax.ShapeDtypeStruct((HALF, 128), jnp.float32),
        in_specs=[pl.BlockSpec(memory_space=pltpu.VMEM)] * 5,
        out_specs=pl.BlockSpec(memory_space=pltpu.VMEM),
        scratch_shapes=[pltpu.VMEM((48 * MODES, 128), jnp.float32)] + [big] * 6,
        compiler_params=pltpu.CompilerParams(vmem_limit_bytes=40 * 2**20),
        cost_estimate=pl.CostEstimate(flops=400_000_000, bytes_accessed=400_000, transcendentals=430_000),
        name="tile_gradient",
    )(points, gen_t, col_parts, row_parts, x)


def assemble_kernel(tiles_ref, out_ref):
    left = lax.broadcasted_iota(jnp.int32, (1, 128), 1) < TILE
    for m in range(SAMPLES // 2):
        a, b = tiles_ref[2 * m], tiles_ref[2 * m + 1]
        out_ref[:HALF, 128 * m : 128 * m + 128] = jnp.where(left, a, pltpu.roll(b, TILE, 1))
        out_ref[HALF:, 128 * m : 128 * m + 128] = jnp.where(left, pltpu.roll(a, TILE, 1), b)


def assemble(tiles):
    return pl.pallas_call(
        assemble_kernel,
        out_shape=jax.ShapeDtypeStruct((TILE, SAMPLES * TILE), jnp.float32),
        in_specs=[pl.BlockSpec(memory_space=pltpu.VMEM)],
        out_specs=pl.BlockSpec(memory_space=pltpu.VMEM),
        compiler_params=pltpu.CompilerParams(vmem_limit_bytes=16 * 2**20),
        name="assemble",
    )(tiles)


def tables_for_tile(tile, first_row, grid_rows, width):
    scale, by_rank = mode_scale(MODES)
    j = jnp.arange(48, dtype=jnp.int32)
    columns = (TILE * tile - HALO + j) % width
    cols = [sine_table((columns + h * HALF) % width, MODES, width).T * by_rank for h in (0, 1)]
    high, low = split(jnp.concatenate(cols, axis=1))
    col_parts = jnp.concatenate([high, high, low], axis=1)
    places = (first_row - 8 + jnp.arange(TALL, dtype=jnp.int32)) % grid_rows
    high, low = split(sine_table(places, MODES, grid_rows).T * (by_rank * scale))
    row_parts = jnp.concatenate([high, high, low], axis=1)
    return col_parts, row_parts


def diffuse(coef, field):
    middle = field[1:-1]
    center = coef[1:-1]
    total = 0.5 * (center + coef[:-2]) * (field[:-2] - middle)
    total = total + 0.5 * (center + coef[2:]) * (field[2:] - middle)
    total = total + 0.5 * (center + jnp.roll(center, 1, -1)) * (jnp.roll(middle, 1, -1) - middle)
    total = total + 0.5 * (center + jnp.roll(center, -1, -1)) * (jnp.roll(middle, -1, -1) - middle)
    return total


def own_final_state(initial_state, control, before, after, point, generator, first_row, grid_rows):
    rows, width = initial_state.shape
    h = STEPS
    cells = point[:, None] * generator % 65536
    scale, by_rank = mode_scale(MODES)
    coeff = (cells.astype(jnp.float32) / 65536.0 - 0.5) * (scale * by_rank[:, None] * by_rank[None, :])
    col_table = sine_table(jnp.arange(width, dtype=jnp.int32), MODES, width)
    inner = jnp.dot(coeff, col_table, precision=lax.Precision.HIGHEST)
    places = (first_row - h + jnp.arange(rows + 2 * h, dtype=jnp.int32)) % grid_rows
    table = sine_table(places, MODES, grid_rows)
    coef = 1.0 + 0.8 * jnp.tanh(jnp.dot(table.T, inner, precision=lax.Precision.HIGHEST))
    state = jnp.concatenate([before[:h], initial_state, after[:h]], axis=0)
    source = jnp.concatenate([before[h:], control, after[h:]], axis=0)
    for step in range(STEPS):
        state = state[1:-1] + DT * (diffuse(coef, state) + source)
        coef, source = coef[1:-1], source[1:-1]
    return state


def strip_shift(step):
    pairs = []
    for samp in range(64):
        for strip in range(4):
            to = (strip + step) % 4
            other = samp if to // 2 == strip // 2 else samp ^ 2
            pairs.append((samp * 4 + strip, other * 4 + to))
    return pairs


RING_UP = [(i, (i + 1) % 4) for i in range(4)]
RING_DOWN = [(j, i) for i, j in RING_UP]


def on_device(initial_state, target, control, point_index, generator):
    rows, width = initial_state.shape
    grid_rows = rows * lax.axis_size("strip")
    tile = lax.axis_index("samp")
    first_row = lax.axis_index("strip") * rows

    own = own_windows((initial_state, control, target), tile)
    above = lax.ppermute(own[:, -8:], "strip", RING_UP)
    below = lax.ppermute(own[:, :8], "strip", RING_DOWN)
    lane = jnp.arange(128, dtype=jnp.int32)[None, :]
    points = lax.psum(jnp.where(lane % SAMPLES == tile, point_index[:, None], 0), "samp")
    col_parts, row_parts = tables_for_tile(tile, first_row, grid_rows, width)
    x = jnp.concatenate([above, own, below], axis=1)
    mine = tile_gradient(points, generator.T, col_parts, row_parts, x)

    tiles = jnp.broadcast_to(mine[None], (4, HALF, 128))
    tiles = lax.all_to_all(tiles, "samp", 0, 0, axis_index_groups=ALONG_Z, tiled=True)
    tiles = jnp.broadcast_to(tiles[None], (16, 4, HALF, 128))
    tiles = lax.all_to_all(tiles, "samp", 0, 0, axis_index_groups=ALONG_XY, tiled=True)
    new_control = assemble(tiles.reshape(SAMPLES, HALF, 128))

    tail = jnp.concatenate([initial_state[-STEPS:], control[1 - STEPS :]], axis=0)
    head = jnp.concatenate([initial_state[:STEPS], control[: STEPS - 1]], axis=0)
    before = lax.ppermute(tail, ("samp", "strip"), strip_shift(1))
    after = lax.ppermute(head, ("samp", "strip"), strip_shift(-1))
    state = own_final_state(initial_state, control, before, after, point_index, generator, first_row, grid_rows)
    return (new_control, state[None])


def solution(mesh):
    placed = (P("strip", None), P("strip", None), P("strip", None), P("samp"), P())
    return jax.shard_map(
        on_device,
        mesh=mesh,
        in_specs=placed,
        out_specs=(P("strip", None), P("samp", "strip", None)),
        check_vma=False,
    )
```

```python
import jax
import jax.numpy as jnp
import numpy as np
from jax import lax
from jax.experimental import pallas as pl
from jax.experimental.pallas import tpu as pltpu
from jax.sharding import PartitionSpec as P

STEPS = 3
DT = 0.12
REG = 0.1
RATE = 1.0
SAMPLES = 64
MODES = 32
HALO = 2 * STEPS - 1
TILE = 64
HALF = TILE // 2
COLS = HALF + 2 * HALO
TALL = TILE + 16

SAMP = np.arange(64).reshape(4, 4, 4)
ALONG_Z = SAMP.reshape(16, 4).tolist()
ALONG_XY = SAMP.transpose(2, 0, 1).reshape(4, 16).tolist()


RANKS = np.arange(1, MODES + 1)
BY_RANK = (1.0 / np.sqrt(RANKS)).astype(np.float32)
SCALE = np.float32(4.0 / np.sum(1.0 / RANKS))


def split(value):
    high = value.astype(jnp.bfloat16)
    return high, (value - high.astype(jnp.float32)).astype(jnp.bfloat16)


def both_parts(value):
    high = value.astype(jnp.bfloat16)
    low = (value - high.astype(np.float32)).astype(jnp.bfloat16)
    return np.concatenate([high, high, low], axis=1)


def row_tables(grid_rows):
    places = np.arange(-8, grid_rows + 8)[:, None]
    sines = np.sin(2.0 * np.pi * (places * RANKS[None, :] % grid_rows) / grid_rows)
    return both_parts((sines * BY_RANK * SCALE).astype(np.float32))


def rows_of_strip(row_ref):
    first = pl.multiple_of(lax.axis_index("strip") * TILE, TILE)
    return row_ref[pl.ds(first, TALL), :]


def tile_col_tables(width):
    ranks = np.tile(RANKS, 4)[None, :]
    turn = 2.0 * np.pi / width
    coarse = turn * (TILE * np.arange(width // TILE)[:, None] * ranks % width)
    half = np.repeat([0, HALF, 0, HALF], MODES)[None, :]
    fine = turn * ((np.arange(48)[:, None] - HALO + half) * ranks % width)
    scaled = np.tile(BY_RANK, 4)[None, :]
    coarse = np.stack([np.sin(coarse), np.cos(coarse)])
    fine = np.stack([np.sin(fine) * scaled, np.cos(fine) * scaled])
    return coarse.astype(np.float32), fine.astype(np.float32)


def edges_kernel(*refs):
    fields, (own, tail, head), near, wide, sems, wide_sems = refs[:3], refs[3:6], *refs[6:]
    rows, width = fields[0].shape
    blocks = width // 128
    tile = lax.axis_index("samp")
    copies = []
    for f in range(2):
        for n, first in enumerate((rows - 8, 0)):
            copies.append(pltpu.make_async_copy(fields[f].at[first : first + 8, :], wide.at[f, n], wide_sems.at[f, n]))
    for f in range(3):
        for n in range(3):
            block = lax.rem(tile // 2 + (blocks - 1 + n), blocks)
            columns = pl.ds(pl.multiple_of(block * 128, 128), 128)
            copies.append(pltpu.make_async_copy(fields[f].at[:, columns], near.at[f, n], sems.at[f, n]))
    for copy in copies:
        copy.start()
    for copy in copies:
        copy.wait()
    row = lax.broadcasted_iota(jnp.int32, (8, 128), 0)
    for b in range(blocks):
        columns = slice(128 * b, 128 * b + 128)
        tail[b] = jnp.where(row >= 8 - STEPS, wide[0, 0, :, columns], pltpu.roll(wide[1, 0, :, columns], 5, 0))
        head[b] = jnp.where(row < STEPS, wide[0, 1, :, columns], pltpu.roll(wide[1, 1, :, columns], 3, 0))
    odd = lax.rem(tile, 2) == 1
    for f in range(3):
        line = jnp.concatenate([near[f, n] for n in range(3)], axis=1)
        even_part = line[:, 128 - HALO : 256 - HALO]
        odd_part = line[:, 192 - HALO : 320 - HALO]
        part = jnp.where(odd, odd_part, even_part)
        own[f] = part
        tail[blocks + f] = part[-8:]
        head[blocks + f] = part[:8]


def own_edges(fields):
    rows, width = fields[0].shape
    vmem = pl.BlockSpec(memory_space=pltpu.VMEM)
    payload = jax.ShapeDtypeStruct((width // 128 + 3, 8, 128), jnp.float32)
    return pl.pallas_call(
        edges_kernel,
        out_shape=[jax.ShapeDtypeStruct((3, rows, 128), jnp.float32), payload, payload],
        in_specs=[pl.BlockSpec(memory_space=pl.ANY)] * 3,
        out_specs=[vmem] * 3,
        scratch_shapes=[
            pltpu.VMEM((3, 3, rows, 128), jnp.float32),
            pltpu.VMEM((2, 2, 8, width), jnp.float32),
            pltpu.SemaphoreType.DMA((3, 3)),
            pltpu.SemaphoreType.DMA((2, 2)),
        ],
        compiler_params=pltpu.CompilerParams(vmem_limit_bytes=56 * 2**20),
        name="own_edges",
    )(*fields)


def tile_kernel(points_ref, gen_ref, coarse_ref, fine_ref, row_ref, above_ref, own_ref, below_ref, out_ref, inner_ref, kx_ref, ky_ref, v_ref, g_ref, t_ref, s_ref):
    f32 = jnp.float32
    lane = lax.broadcasted_iota(jnp.int32, (1, 128), 1)
    left = lane < SAMPLES
    edge = above_ref.shape[0] - 3
    tile = lax.axis_index("samp")
    sines = coarse_ref[0, pl.ds(tile, 1), :] * fine_ref[1] + coarse_ref[1, pl.ds(tile, 1), :] * fine_ref[0]
    high, low = split(sines)
    col_parts = jnp.concatenate([high, low[:, : 2 * MODES]], axis=1)
    row_parts = rows_of_strip(row_ref)

    sample = lax.broadcasted_iota(jnp.int32, (SAMPLES, 128), 0)
    points = jnp.sum(jnp.where(sample == lane % SAMPLES, points_ref[...], 0), axis=0, keepdims=True)
    for p in range(MODES):
        cells = (points * gen_ref[:, p : p + 1]) & 65535
        coords = cells.astype(f32) * (1.0 / 65536.0) - 0.5
        both = jnp.concatenate([jnp.where(left, coords, 0.0), jnp.where(left, 0.0, coords)], axis=0)
        high, low = split(both)
        inner_ref[48 * p : 48 * p + 48, :] = jnp.dot(
            col_parts, jnp.concatenate([high, low, high], axis=0), preferred_element_type=f32
        )

    start_fields = []
    for f in range(3):
        x = jnp.concatenate([above_ref[edge + f], own_ref[f], below_ref[edge + f]], axis=0)
        start_fields.append(x * DT if f == 1 else x)
    before = jnp.zeros((TALL, 128), f32)
    for j in range(COLS):
        high, low = split(inner_ref[pl.ds(j, MODES, stride=48), :])
        log = jnp.dot(row_parts, jnp.concatenate([high, low, high], axis=0), preferred_element_type=f32)
        k = 0.5 * DT + (0.5 * DT * 0.8) * jnp.tanh(log)
        kx_ref[j] = before + k
        ky_ref[j] = k + pltpu.roll(k, TALL - 1, 0)
        before = k
        for x, ref in zip(start_fields, (v_ref, g_ref, t_ref)):
            ref[j] = jnp.where(left, x[:, j : j + 1], x[:, j + HALF : j + HALF + 1])

    def divergence(j, carry):
        v, left_flux = carry
        right = v_ref[j + 1]
        right_flux = kx_ref[j + 1] * (right - v)
        down_flux = ky_ref[j] * (pltpu.roll(v, TALL - 1, 0) - v)
        new = v + ((right_flux - left_flux) + (down_flux - pltpu.roll(down_flux, 1, 0)))
        return new, (right, right_flux)

    def sweep(first, body):
        v = v_ref[first]
        start = (v, kx_ref[first] * (v - v_ref[first - 1]))
        return start, first, COLS - first

    def state_step(j, carry):
        new, after = divergence(j, carry)
        v_ref[j] = new + g_ref[j]
        return after

    def last_state_step(j, carry):
        new, after = divergence(j, carry)
        v_ref[j] = new + g_ref[j] - t_ref[j]
        return after

    def first_costate_step(j, carry):
        new, after = divergence(j, carry)
        s_ref[j] = carry[0] + new
        v_ref[j] = new
        return after

    for t, body in enumerate((state_step, state_step, last_state_step, first_costate_step)):
        start, low_j, high_j = sweep(t + 1, body)
        lax.fori_loop(low_j, high_j, body, start, unroll=2)

    source = lax.broadcasted_iota(jnp.int32, (256, 128), 0) % 128 // SAMPLES
    place = lax.broadcasted_iota(jnp.int32, (256, 128), 1) // HALF % 2
    add_samples = (source == place).astype(f32).astype(jnp.bfloat16)

    def last_costate_step(j, carry):
        total, carry = carry
        new, after = divergence(j, carry)
        high, low = split((s_ref[j] + new)[8 : 8 + TILE])
        sums = jnp.dot(jnp.concatenate([high, low], axis=1), add_samples, preferred_element_type=f32)
        return jnp.where(lane % HALF == j - HALO, sums, total), after

    start, low_j, high_j = sweep(HALO, last_costate_step)
    total, _ = lax.fori_loop(low_j, high_j, last_costate_step, (jnp.zeros((TILE, 128), f32), start), unroll=16)

    total = jnp.where(left, total[:HALF], total[HALF:])
    control = own_ref[1]
    top = pltpu.roll(control[:HALF], 128 - HALO, 1)
    bottom = pltpu.roll(control[HALF:], TILE - HALO, 1)
    control = jnp.where(left, top, bottom)
    out_ref[...] = control - RATE * (total * (DT / SAMPLES) + REG * control)


def tile_gradient(*args):
    big = pltpu.VMEM((COLS, TALL, 128), jnp.float32)
    return pl.pallas_call(
        tile_kernel,
        out_shape=jax.ShapeDtypeStruct((HALF, 128), jnp.float32),
        in_specs=[pl.BlockSpec(memory_space=pltpu.VMEM)] * len(args),
        out_specs=pl.BlockSpec(memory_space=pltpu.VMEM),
        scratch_shapes=[pltpu.VMEM((48 * MODES, 128), jnp.float32)] + [big] * 6,
        compiler_params=pltpu.CompilerParams(vmem_limit_bytes=40 * 2**20),
        cost_estimate=pl.CostEstimate(flops=400_000_000, bytes_accessed=400_000, transcendentals=430_000),
        name="tile_gradient",
    )(*args)


def assemble_kernel(tiles_ref, out_ref):
    left = lax.broadcasted_iota(jnp.int32, (1, 128), 1) < TILE
    z = lax.rem(lax.axis_index("samp"), 4)
    for m in range(SAMPLES // 2):
        near = 4 * (m // 2)
        a = tiles_ref[near + lax.rem(z + (4 - 2 * m % 4), 4)]
        b = tiles_ref[near + lax.rem(z + (3 - 2 * m % 4), 4)]
        out_ref[:HALF, 128 * m : 128 * m + 128] = jnp.where(left, a, pltpu.roll(b, TILE, 1))
        out_ref[HALF:, 128 * m : 128 * m + 128] = jnp.where(left, pltpu.roll(a, TILE, 1), b)


def assemble(tiles):
    return pl.pallas_call(
        assemble_kernel,
        out_shape=jax.ShapeDtypeStruct((TILE, SAMPLES * TILE), jnp.float32),
        in_specs=[pl.BlockSpec(memory_space=pltpu.VMEM)],
        out_specs=pl.BlockSpec(memory_space=pltpu.VMEM),
        compiler_params=pltpu.CompilerParams(vmem_limit_bytes=16 * 2**20),
        name="assemble",
    )(tiles)


def state_kernel(point_ref, gen_ref, row_ref, coarse_ref, fine_ref, init_ref, control_ref, before_ref, after_ref, out_ref, kx_ref, ky_ref, g_ref, v_ref, w_ref):
    f32 = jnp.float32
    blocks = v_ref.shape[0]
    lane = lax.broadcasted_iota(jnp.int32, (1, 128), 1)
    first, last = lane == 0, lane == 127

    cells = (point_ref[0] * gen_ref[...]) & 65535
    high, low = split(cells.astype(f32) * (1.0 / 65536.0) - 0.5)
    coords = jnp.concatenate([high, high, low], axis=1)

    rows, above = out_ref.shape[0], 8
    row_parts = rows_of_strip(row_ref)

    def to_left(value):
        return pltpu.roll(value, 127, 1)

    def up(value):
        return pltpu.roll(value, value.shape[0] - 1, 0)

    before_k, before_shifted, first_shifted = None, None, None
    for b in range(blocks):
        sine = coarse_ref[0][:, b : b + 1] * fine_ref[1] + coarse_ref[1][:, b : b + 1] * fine_ref[0]
        high, low = split(sine)
        inner = jnp.dot(coords, jnp.concatenate([high, low, high], axis=0), preferred_element_type=f32)
        high, low = split(inner)
        log = jnp.dot(row_parts, jnp.concatenate([high, low, high], axis=0), preferred_element_type=f32)
        k = 0.5 * DT + (0.5 * DT * 0.8) * jnp.tanh(log)
        ky_ref[b] = k + up(k)
        shifted = to_left(k)
        if b == 0:
            first_shifted = shifted
        else:
            kx_ref[b - 1] = before_k + jnp.where(last, shifted, before_shifted)
        before_k, before_shifted = k, shifted
        columns = slice(128 * b, 128 * b + 128)
        lead, trail = before_ref[b], after_ref[b]
        v_ref[b] = jnp.concatenate([lead, init_ref[:, columns], trail], axis=0)
        g_ref[b] = DT * jnp.concatenate([pltpu.roll(lead, 3, 0), control_ref[:, columns], pltpu.roll(trail, 5, 0)], axis=0)
    kx_ref[blocks - 1] = before_k + jnp.where(last, first_shifted, before_shifted)

    def sweep(source, write):
        v = source[blocks - 1]
        flux = kx_ref[blocks - 1] * (jnp.where(last, to_left(source[0]), to_left(v)) - v)
        start = (source[0], to_left(source[0]), pltpu.roll(flux, 1, 1))

        def step(b, carry):
            v, shifted, flux_before = carry
            following = source[lax.rem(b + 1, blocks)]
            following_shifted = to_left(following)
            flux = kx_ref[b] * (jnp.where(last, following_shifted, shifted) - v)
            flux_shifted = pltpu.roll(flux, 1, 1)
            down = ky_ref[b] * (up(v) - v)
            new = v + ((flux - jnp.where(first, flux_before, flux_shifted)) + (down - pltpu.roll(down, 1, 0)))
            write(b, new + g_ref[b])
            return following, following_shifted, flux_shifted

        lax.fori_loop(0, blocks, step, start, unroll=2)

    def keep(ref):
        def write(b, value):
            ref[b] = value
        return write

    def finish(b, value):
        out_ref[:, pl.ds(pl.multiple_of(b * 128, 128), 128)] = value[above : above + rows]

    sweep(v_ref, keep(w_ref))
    sweep(w_ref, keep(v_ref))
    sweep(v_ref, finish)


def own_final_state(point_index, generator, row_table, initial_state, control, before, after):
    rows, width = initial_state.shape
    blocks = width // 128
    turns = 2.0 * np.pi / width * RANKS[:, None]
    coarse = turns * (128 * np.arange(blocks))[None, :]
    fine = turns * np.arange(128)[None, :]
    scaled = BY_RANK[:, None]
    coarse = np.stack([np.sin(coarse), np.cos(coarse)]).astype(np.float32)
    fine = np.stack([np.sin(fine) * scaled, np.cos(fine) * scaled]).astype(np.float32)
    big = pltpu.VMEM((blocks, rows + 16, 128), jnp.float32)
    return pl.pallas_call(
        state_kernel,
        out_shape=jax.ShapeDtypeStruct((rows, width), jnp.float32),
        in_specs=[pl.BlockSpec(memory_space=pltpu.SMEM)] + [pl.BlockSpec(memory_space=pltpu.VMEM)] * 8,
        out_specs=pl.BlockSpec(memory_space=pltpu.VMEM),
        scratch_shapes=[big] * 5,
        compiler_params=pltpu.CompilerParams(vmem_limit_bytes=40 * 2**20),
        cost_estimate=pl.CostEstimate(flops=2_000_000_000, bytes_accessed=3_500_000, transcendentals=330_000),
        name="own_final_state",
    )(point_index, generator, row_table, coarse, fine, initial_state, control, before, after)


RING_UP = [(i, (i + 1) % 4) for i in range(4)]
RING_DOWN = [(j, i) for i, j in RING_UP]


def z_shift(step):
    return [(i, i // 4 * 4 + (i + step) % 4) for i in range(64)]


def on_device(initial_state, target, control, point_index, generator):
    rows, width = initial_state.shape
    row_table = row_tables(rows * lax.axis_size("strip"))

    own, tail, head = own_edges((initial_state, control, target))
    point_index, tail, head = lax.optimization_barrier((point_index, tail, head))
    above = lax.ppermute(tail, "strip", RING_UP)
    below = lax.ppermute(head, "strip", RING_DOWN)
    points = jnp.broadcast_to(point_index[:, None, None], (SAMPLES, 1, 128))
    points = lax.all_to_all(points, "samp", 0, 0, tiled=True).reshape(SAMPLES, 128)
    mine = tile_gradient(points, generator.T, *tile_col_tables(width), row_table, above, own, below)

    tiles = jnp.stack([mine] + [lax.ppermute(mine, "samp", z_shift(k)) for k in (1, 2, 3)])
    tiles = jnp.broadcast_to(tiles[None], (16, 4, HALF, 128))
    tiles, generator = lax.optimization_barrier((tiles, generator))
    tiles = lax.all_to_all(tiles, "samp", 0, 0, axis_index_groups=ALONG_XY, tiled=True)
    new_control = assemble(tiles.reshape(SAMPLES, HALF, 128))

    state = own_final_state(point_index, generator, row_table, initial_state, control, above, below)
    return (new_control, state[None])


def solution(mesh):
    placed = (P("strip", None), P("strip", None), P("strip", None), P("samp"), P())
    return jax.shard_map(
        on_device,
        mesh=mesh,
        in_specs=placed,
        out_specs=(P("strip", None), P("samp", "strip", None)),
        check_vma=False,
    )
```

```python
import jax
import jax.numpy as jnp
import numpy as np
from jax import lax
from jax.experimental import pallas as pl
from jax.experimental.pallas import tpu as pltpu
from jax.sharding import PartitionSpec as P

STEPS = 3
DT = 0.12
REG = 0.1
RATE = 1.0
SAMPLES = 64
MODES = 32
HALO = 2 * STEPS - 1
TILE = 64
HALF = TILE // 2
COLS = HALF + 2 * HALO
TALL = TILE + 16

SAMP = np.arange(64).reshape(4, 4, 4)
ALONG_Z = SAMP.reshape(16, 4).tolist()
ALONG_XY = SAMP.transpose(2, 0, 1).reshape(4, 16).tolist()


RANKS = np.arange(1, MODES + 1)
BY_RANK = (1.0 / np.sqrt(RANKS)).astype(np.float32)
SCALE = np.float32(4.0 / np.sum(1.0 / RANKS))


def split(value):
    high = value.astype(jnp.bfloat16)
    return high, (value - high.astype(jnp.float32)).astype(jnp.bfloat16)


def both_parts(value):
    high = value.astype(jnp.bfloat16)
    low = (value - high.astype(np.float32)).astype(jnp.bfloat16)
    return np.concatenate([high, high, low], axis=1)


def row_tables(grid_rows):
    places = np.arange(-8, grid_rows + 8)[:, None]
    sines = np.sin(2.0 * np.pi * (places * RANKS[None, :] % grid_rows) / grid_rows)
    return both_parts((sines * BY_RANK * SCALE).astype(np.float32))


def rows_of_strip(row_ref):
    first = pl.multiple_of(lax.axis_index("strip") * TILE, TILE)
    return row_ref[pl.ds(first, TALL), :]


def tile_col_tables(width):
    ranks = np.tile(RANKS, 4)[None, :]
    turn = 2.0 * np.pi / width
    coarse = turn * (TILE * np.arange(width // TILE)[:, None] * ranks % width)
    half = np.repeat([0, HALF, 0, HALF], MODES)[None, :]
    fine = turn * ((np.arange(48)[:, None] - HALO + half) * ranks % width)
    scaled = np.tile(BY_RANK, 4)[None, :]
    coarse = np.stack([np.sin(coarse), np.cos(coarse)])
    fine = np.stack([np.sin(fine) * scaled, np.cos(fine) * scaled])
    return coarse.astype(np.float32), fine.astype(np.float32)


def window_of(parts, tile):
    line = jnp.concatenate(parts, axis=1)
    even_part = line[:, 128 - HALO : 256 - HALO]
    odd_part = line[:, 192 - HALO : 320 - HALO]
    return jnp.where(lax.rem(tile, 2) == 1, odd_part, even_part)


def edge_rows(rows):
    odd = lax.rem(lax.axis_index("strip"), 2)
    return pl.multiple_of((1 - odd) * (rows - 8), 8), pl.multiple_of(odd * (rows - 8), 8)


def edges_kernel(*refs):
    fields, (own, to_core, to_z, wide_to_core, wide_to_z), near, edge, sems, edge_sems = refs[:3], refs[3:8], *refs[8:]
    rows, width = fields[0].shape
    blocks = width // 128
    tile = lax.axis_index("samp")
    firsts = edge_rows(rows)

    def column_block(t, n):
        block = lax.rem(t // 2 + (blocks - 1 + n), blocks)
        return pl.ds(pl.multiple_of(block * 128, 128), 128)

    copies = []
    for n in range(2):
        for f in range(3):
            copies.append(pltpu.make_async_copy(fields[f].at[pl.ds(firsts[n], 8), :], edge.at[f, n], edge_sems.at[f, n]))
    for f in range(3):
        for n in range(3):
            copies.append(pltpu.make_async_copy(fields[f].at[:, column_block(tile, n)], near.at[f, n], sems.at[f, n]))
    for copy in copies:
        copy.start()
    for copy in copies:
        copy.wait()

    odd = lax.rem(lax.axis_index("strip"), 2)
    for f in range(3):
        own[f] = window_of([near[f, n] for n in range(3)], tile)
        for n, (out, partner) in enumerate(((to_core, tile), (to_z, tile ^ 2))):
            out[f] = window_of([edge[f, n, :, column_block(partner, m)] for m in range(3)], tile)
    row = lax.broadcasted_iota(jnp.int32, (8, 128), 0)
    for n, out in enumerate((wide_to_core, wide_to_z)):
        is_tail = odd == n
        is_state = jnp.where(is_tail, row, 7 - row) >= 8 - STEPS
        for b in range(blocks):
            columns = slice(128 * b, 128 * b + 128)
            source = edge[1, n, :, columns]
            moved = jnp.where(is_tail, pltpu.roll(source, 5, 0), pltpu.roll(source, 3, 0))
            out[b] = jnp.where(is_state, edge[0, n, :, columns], moved)


def strip_edges(fields):
    rows, width = fields[0].shape
    vmem = pl.BlockSpec(memory_space=pltpu.VMEM)
    shapes = [(3, rows, 128), (3, 8, 128), (3, 8, 128), (width // 128, 8, 128), (width // 128, 8, 128)]
    return pl.pallas_call(
        edges_kernel,
        out_shape=[jax.ShapeDtypeStruct(shape, jnp.float32) for shape in shapes],
        in_specs=[pl.BlockSpec(memory_space=pl.ANY)] * 3,
        out_specs=[vmem] * 5,
        scratch_shapes=[
            pltpu.VMEM((3, 3, rows, 128), jnp.float32),
            pltpu.VMEM((3, 2, 8, width), jnp.float32),
            pltpu.SemaphoreType.DMA((3, 3)),
            pltpu.SemaphoreType.DMA((3, 2)),
        ],
        compiler_params=pltpu.CompilerParams(vmem_limit_bytes=56 * 2**20),
        name="strip_edges",
    )(*fields)


def tile_kernel(points_ref, gen_ref, coarse_ref, fine_ref, row_ref, core_ref, own_ref, z_ref, out_ref, inner_ref, kx_ref, ky_ref, v_ref, g_ref, t_ref, s_ref):
    f32 = jnp.float32
    lane = lax.broadcasted_iota(jnp.int32, (1, 128), 1)
    left = lane < SAMPLES
    odd = lax.rem(lax.axis_index("strip"), 2) == 1
    tile = lax.axis_index("samp")
    sines = coarse_ref[0, pl.ds(tile, 1), :] * fine_ref[1] + coarse_ref[1, pl.ds(tile, 1), :] * fine_ref[0]
    high, low = split(sines)
    col_parts = jnp.concatenate([high, low[:, : 2 * MODES]], axis=1)
    row_parts = rows_of_strip(row_ref)

    sample = lax.broadcasted_iota(jnp.int32, (SAMPLES, 128), 0)
    points = jnp.sum(jnp.where(sample == lane % SAMPLES, points_ref[...], 0), axis=0, keepdims=True)
    for p in range(MODES):
        cells = (points * gen_ref[:, p : p + 1]) & 65535
        coords = cells.astype(f32) * (1.0 / 65536.0) - 0.5
        both = jnp.concatenate([jnp.where(left, coords, 0.0), jnp.where(left, 0.0, coords)], axis=0)
        high, low = split(both)
        inner_ref[48 * p : 48 * p + 48, :] = jnp.dot(
            col_parts, jnp.concatenate([high, low, high], axis=0), preferred_element_type=f32
        )

    start_fields = []
    for f in range(3):
        core, far = core_ref[f], z_ref[f]
        x = jnp.concatenate([jnp.where(odd, core, far), own_ref[f], jnp.where(odd, far, core)], axis=0)
        start_fields.append(x * DT if f == 1 else x)
    before = jnp.zeros((TALL, 128), f32)
    for j in range(COLS):
        high, low = split(inner_ref[pl.ds(j, MODES, stride=48), :])
        log = jnp.dot(row_parts, jnp.concatenate([high, low, high], axis=0), preferred_element_type=f32)
        k = 0.5 * DT + (0.5 * DT * 0.8) * jnp.tanh(log)
        kx_ref[j] = before + k
        ky_ref[j] = k + pltpu.roll(k, TALL - 1, 0)
        before = k
        for x, ref in zip(start_fields, (v_ref, g_ref, t_ref)):
            ref[j] = jnp.where(left, x[:, j : j + 1], x[:, j + HALF : j + HALF + 1])

    def divergence(j, carry):
        v, left_flux = carry
        right = v_ref[j + 1]
        right_flux = kx_ref[j + 1] * (right - v)
        down_flux = ky_ref[j] * (pltpu.roll(v, TALL - 1, 0) - v)
        new = v + ((right_flux - left_flux) + (down_flux - pltpu.roll(down_flux, 1, 0)))
        return new, (right, right_flux)

    def sweep(first, body):
        v = v_ref[first]
        start = (v, kx_ref[first] * (v - v_ref[first - 1]))
        return start, first, COLS - first

    def state_step(j, carry):
        new, after = divergence(j, carry)
        v_ref[j] = new + g_ref[j]
        return after

    def last_state_step(j, carry):
        new, after = divergence(j, carry)
        v_ref[j] = new + g_ref[j] - t_ref[j]
        return after

    def first_costate_step(j, carry):
        new, after = divergence(j, carry)
        s_ref[j] = carry[0] + new
        v_ref[j] = new
        return after

    for t, body in enumerate((state_step, state_step, last_state_step, first_costate_step)):
        start, low_j, high_j = sweep(t + 1, body)
        lax.fori_loop(low_j, high_j, body, start, unroll=8)

    source = lax.broadcasted_iota(jnp.int32, (256, 128), 0) % 128 // SAMPLES
    place = lax.broadcasted_iota(jnp.int32, (256, 128), 1) // HALF % 2
    add_samples = (source == place).astype(f32).astype(jnp.bfloat16)

    def last_costate_step(j, carry):
        total, carry = carry
        new, after = divergence(j, carry)
        high, low = split((s_ref[j] + new)[8 : 8 + TILE])
        sums = jnp.dot(jnp.concatenate([high, low], axis=1), add_samples, preferred_element_type=f32)
        return jnp.where(lane % HALF == j - HALO, sums, total), after

    start, low_j, high_j = sweep(HALO, last_costate_step)
    total, _ = lax.fori_loop(low_j, high_j, last_costate_step, (jnp.zeros((TILE, 128), f32), start), unroll=32)

    total = jnp.where(left, total[:HALF], total[HALF:])
    control = own_ref[1]
    top = pltpu.roll(control[:HALF], 128 - HALO, 1)
    bottom = pltpu.roll(control[HALF:], TILE - HALO, 1)
    control = jnp.where(left, top, bottom)
    out_ref[...] = control - RATE * (total * (DT / SAMPLES) + REG * control)


def tile_gradient(*args):
    big = pltpu.VMEM((COLS, TALL, 128), jnp.float32)
    return pl.pallas_call(
        tile_kernel,
        out_shape=jax.ShapeDtypeStruct((HALF, 128), jnp.float32),
        in_specs=[pl.BlockSpec(memory_space=pltpu.VMEM)] * len(args),
        out_specs=pl.BlockSpec(memory_space=pltpu.VMEM),
        scratch_shapes=[pltpu.VMEM((48 * MODES, 128), jnp.float32)] + [big] * 6,
        compiler_params=pltpu.CompilerParams(vmem_limit_bytes=40 * 2**20),
        cost_estimate=pl.CostEstimate(flops=4_000_000_000, bytes_accessed=20_000_000, transcendentals=430_000),
        name="tile_gradient",
    )(*args)


def assemble_kernel(tiles_ref, out_ref):
    left = lax.broadcasted_iota(jnp.int32, (1, 128), 1) < TILE
    z = lax.rem(lax.axis_index("samp"), 4)
    for m in range(SAMPLES // 2):
        near = 4 * (m // 2)
        a = tiles_ref[near + (z ^ (2 * m % 4))]
        b = tiles_ref[near + (z ^ (2 * m % 4 + 1))]
        out_ref[:HALF, 128 * m : 128 * m + 128] = jnp.where(left, a, pltpu.roll(b, TILE, 1))
        out_ref[HALF:, 128 * m : 128 * m + 128] = jnp.where(left, pltpu.roll(a, TILE, 1), b)


def assemble(tiles):
    return pl.pallas_call(
        assemble_kernel,
        out_shape=jax.ShapeDtypeStruct((TILE, SAMPLES * TILE), jnp.float32),
        in_specs=[pl.BlockSpec(memory_space=pltpu.VMEM)],
        out_specs=pl.BlockSpec(memory_space=pltpu.VMEM),
        compiler_params=pltpu.CompilerParams(vmem_limit_bytes=16 * 2**20),
        name="assemble",
    )(tiles)


def state_kernel(point_ref, gen_ref, row_ref, coarse_ref, fine_ref, init_ref, control_ref, core_ref, z_ref, out_ref, kx_ref, ky_ref, g_ref, v_ref, w_ref):
    f32 = jnp.float32
    blocks = v_ref.shape[0]
    lane = lax.broadcasted_iota(jnp.int32, (1, 128), 1)
    first, last = lane == 0, lane == 127

    cells = (point_ref[0] * gen_ref[...]) & 65535
    high, low = split(cells.astype(f32) * (1.0 / 65536.0) - 0.5)
    coords = jnp.concatenate([high, high, low], axis=1)

    rows, above = out_ref.shape[0], 8
    row_parts = rows_of_strip(row_ref)
    odd = lax.rem(lax.axis_index("strip"), 2) == 1

    def to_left(value):
        return pltpu.roll(value, 127, 1)

    def up(value):
        return pltpu.roll(value, value.shape[0] - 1, 0)

    before_k, before_shifted, first_shifted = None, None, None
    for b in range(blocks):
        sine = coarse_ref[0][:, b : b + 1] * fine_ref[1] + coarse_ref[1][:, b : b + 1] * fine_ref[0]
        high, low = split(sine)
        inner = jnp.dot(coords, jnp.concatenate([high, low, high], axis=0), preferred_element_type=f32)
        high, low = split(inner)
        log = jnp.dot(row_parts, jnp.concatenate([high, low, high], axis=0), preferred_element_type=f32)
        k = 0.5 * DT + (0.5 * DT * 0.8) * jnp.tanh(log)
        ky_ref[b] = k + up(k)
        shifted = to_left(k)
        if b == 0:
            first_shifted = shifted
        else:
            kx_ref[b - 1] = before_k + jnp.where(last, shifted, before_shifted)
        before_k, before_shifted = k, shifted
        columns = slice(128 * b, 128 * b + 128)
        core, far = core_ref[b], z_ref[b]
        lead, trail = jnp.where(odd, core, far), jnp.where(odd, far, core)
        v_ref[b] = jnp.concatenate([lead, init_ref[:, columns], trail], axis=0)
        g_ref[b] = DT * jnp.concatenate([pltpu.roll(lead, 3, 0), control_ref[:, columns], pltpu.roll(trail, 5, 0)], axis=0)
    kx_ref[blocks - 1] = before_k + jnp.where(last, first_shifted, before_shifted)

    def sweep(source, write):
        v = source[blocks - 1]
        flux = kx_ref[blocks - 1] * (jnp.where(last, to_left(source[0]), to_left(v)) - v)
        start = (source[0], to_left(source[0]), pltpu.roll(flux, 1, 1))

        def step(b, carry):
            v, shifted, flux_before = carry
            following = source[lax.rem(b + 1, blocks)]
            following_shifted = to_left(following)
            flux = kx_ref[b] * (jnp.where(last, following_shifted, shifted) - v)
            flux_shifted = pltpu.roll(flux, 1, 1)
            down = ky_ref[b] * (up(v) - v)
            new = v + ((flux - jnp.where(first, flux_before, flux_shifted)) + (down - pltpu.roll(down, 1, 0)))
            write(b, new + g_ref[b])
            return following, following_shifted, flux_shifted

        lax.fori_loop(0, blocks, step, start, unroll=8)

    def keep(ref):
        def write(b, value):
            ref[b] = value
        return write

    def finish(b, value):
        out_ref[:, pl.ds(pl.multiple_of(b * 128, 128), 128)] = value[above : above + rows]

    sweep(v_ref, keep(w_ref))
    sweep(w_ref, keep(v_ref))
    sweep(v_ref, finish)


def own_final_state(point_index, generator, row_table, initial_state, control, from_core, from_z):
    rows, width = initial_state.shape
    blocks = width // 128
    turns = 2.0 * np.pi / width * RANKS[:, None]
    coarse = turns * (128 * np.arange(blocks))[None, :]
    fine = turns * np.arange(128)[None, :]
    scaled = BY_RANK[:, None]
    coarse = np.stack([np.sin(coarse), np.cos(coarse)]).astype(np.float32)
    fine = np.stack([np.sin(fine) * scaled, np.cos(fine) * scaled]).astype(np.float32)
    big = pltpu.VMEM((blocks, rows + 16, 128), jnp.float32)
    return pl.pallas_call(
        state_kernel,
        out_shape=jax.ShapeDtypeStruct((rows, width), jnp.float32),
        in_specs=[pl.BlockSpec(memory_space=pltpu.SMEM)] + [pl.BlockSpec(memory_space=pltpu.VMEM)] * 8,
        out_specs=pl.BlockSpec(memory_space=pltpu.VMEM),
        scratch_shapes=[big] * 5,
        compiler_params=pltpu.CompilerParams(vmem_limit_bytes=40 * 2**20),
        cost_estimate=pl.CostEstimate(flops=2_000_000_000, bytes_accessed=3_500_000, transcendentals=330_000),
        name="own_final_state",
    )(point_index, generator, row_table, coarse, fine, initial_state, control, from_core, from_z)


CORES = [(s * 4 + k, s * 4 + (k ^ 1)) for s in range(64) for k in range(4)]
ACROSS = [(s * 4 + k, (s ^ 2) * 4 + 3 - k) for s in range(64) for k in range(4)]


def z_partner(other):
    return [(i, i ^ other) for i in range(64)]


def on_device(initial_state, target, control, point_index, generator):
    rows, width = initial_state.shape
    row_table = row_tables(rows * lax.axis_size("strip"))

    both = ("samp", "strip")
    own, to_core, to_z, wide_to_core, wide_to_z = strip_edges((initial_state, control, target))
    core, far = lax.ppermute(to_core, both, CORES), lax.ppermute(to_z, both, ACROSS)
    core_wide, far_wide = lax.ppermute(wide_to_core, both, CORES), lax.ppermute(wide_to_z, both, ACROSS)
    points = jnp.broadcast_to(point_index[:, None, None], (SAMPLES, 1, 128))
    points = lax.all_to_all(points, "samp", 0, 0, tiled=True).reshape(SAMPLES, 128)
    mine = tile_gradient(points, generator.T, *tile_col_tables(width), row_table, core, own, far)

    mine, core_wide, far_wide = lax.optimization_barrier((mine, core_wide, far_wide))
    tiles = jnp.stack([mine] + [lax.ppermute(mine, "samp", z_partner(k)) for k in (1, 2, 3)])
    tiles = jnp.broadcast_to(tiles[None], (16, 4, HALF, 128))
    tiles, generator = lax.optimization_barrier((tiles, generator))
    tiles = lax.all_to_all(tiles, "samp", 0, 0, axis_index_groups=ALONG_XY, tiled=True)
    new_control = assemble(tiles.reshape(SAMPLES, HALF, 128))

    state = own_final_state(point_index, generator, row_table, initial_state, control, core_wide, far_wide)
    return (new_control, state[None])


def solution(mesh):
    placed = (P("strip", None), P("strip", None), P("strip", None), P("samp"), P())
    return jax.shard_map(
        on_device,
        mesh=mesh,
        in_specs=placed,
        out_specs=(P("strip", None), P("samp", "strip", None)),
        check_vma=False,
    )
```

```python
import jax
import jax.numpy as jnp
import numpy as np
from jax import lax
from jax.experimental import pallas as pl
from jax.experimental.pallas import tpu as pltpu
from jax.sharding import PartitionSpec as P

STEPS = 3
DT = 0.12
REG = 0.1
RATE = 1.0
SAMPLES = 64
MODES = 32
HALO = 2 * STEPS - 1
TILE = 64
HALF = TILE // 2
COLS = HALF + 2 * HALO
TALL = TILE + 16

RANKS = np.arange(1, MODES + 1)
BY_RANK = (1.0 / np.sqrt(RANKS)).astype(np.float32)
SCALE = np.float32(4.0 / np.sum(1.0 / RANKS))


def split(value):
    high = value.astype(jnp.bfloat16)
    return high, (value - high.astype(jnp.float32)).astype(jnp.bfloat16)


def both_parts(value):
    high = value.astype(jnp.bfloat16)
    low = (value - high.astype(np.float32)).astype(jnp.bfloat16)
    return np.concatenate([high, high, low], axis=1)


def row_tables(grid_rows):
    places = np.arange(-8, grid_rows + 8)[:, None]
    sines = np.sin(2.0 * np.pi * (places * RANKS[None, :] % grid_rows) / grid_rows)
    return both_parts((sines * BY_RANK * SCALE).astype(np.float32))


def rows_of_strip(row_ref):
    first = pl.multiple_of(lax.axis_index("strip") * TILE, TILE)
    return row_ref[pl.ds(first, TALL), :]


def tile_col_tables(width):
    ranks = np.tile(RANKS, 4)[None, :]
    turn = 2.0 * np.pi / width
    coarse = turn * (TILE * np.arange(width // TILE)[:, None] * ranks % width)
    half = np.repeat([0, HALF, 0, HALF], MODES)[None, :]
    fine = turn * ((np.arange(48)[:, None] - HALO + half) * ranks % width)
    scaled = np.tile(BY_RANK, 4)[None, :]
    coarse = np.stack([np.sin(coarse), np.cos(coarse)])
    fine = np.stack([np.sin(fine) * scaled, np.cos(fine) * scaled])
    return coarse.astype(np.float32), fine.astype(np.float32)


def window_of(parts, tile):
    line = jnp.concatenate(parts, axis=1)
    even_part = line[:, 128 - HALO : 256 - HALO]
    odd_part = line[:, 192 - HALO : 320 - HALO]
    return jnp.where(lax.rem(tile, 2) == 1, odd_part, even_part)


def edge_rows(rows):
    odd = lax.rem(lax.axis_index("strip"), 2)
    return pl.multiple_of((1 - odd) * (rows - 8), 8), pl.multiple_of(odd * (rows - 8), 8)


def edges_kernel(*refs):
    fields, (own, to_core, to_z, wide_to_core, wide_to_z), near, edge, sems, edge_sems = refs[:3], refs[3:8], *refs[8:]
    rows, width = fields[0].shape
    blocks = width // 128
    tile = lax.axis_index("samp")
    firsts = edge_rows(rows)

    def column_block(t, n):
        block = lax.rem(t // 2 + (blocks - 1 + n), blocks)
        return pl.ds(pl.multiple_of(block * 128, 128), 128)

    copies = []
    for n in range(2):
        for f in range(3):
            copies.append(pltpu.make_async_copy(fields[f].at[pl.ds(firsts[n], 8), :], edge.at[f, n], edge_sems.at[f, n]))
    for f in range(3):
        for n in range(3):
            copies.append(pltpu.make_async_copy(fields[f].at[:, column_block(tile, n)], near.at[f, n], sems.at[f, n]))
    for copy in copies:
        copy.start()
    for copy in copies:
        copy.wait()

    odd = lax.rem(lax.axis_index("strip"), 2)
    for f in range(3):
        own[f] = window_of([near[f, n] for n in range(3)], tile)
        for n, (out, partner) in enumerate(((to_core, tile), (to_z, tile ^ 2))):
            out[f] = window_of([edge[f, n, :, column_block(partner, m)] for m in range(3)], tile)
    row = lax.broadcasted_iota(jnp.int32, (8, 128), 0)
    for n, out in enumerate((wide_to_core, wide_to_z)):
        is_tail = odd == n
        is_state = jnp.where(is_tail, row, 7 - row) >= 8 - STEPS
        for b in range(blocks):
            columns = slice(128 * b, 128 * b + 128)
            source = edge[1, n, :, columns]
            moved = jnp.where(is_tail, pltpu.roll(source, 5, 0), pltpu.roll(source, 3, 0))
            out[b] = jnp.where(is_state, edge[0, n, :, columns], moved)


def strip_edges(fields):
    rows, width = fields[0].shape
    vmem = pl.BlockSpec(memory_space=pltpu.VMEM)
    shapes = [(3, rows, 128), (3, 8, 128), (3, 8, 128), (width // 128, 8, 128), (width // 128, 8, 128)]
    return pl.pallas_call(
        edges_kernel,
        out_shape=[jax.ShapeDtypeStruct(shape, jnp.float32) for shape in shapes],
        in_specs=[pl.BlockSpec(memory_space=pl.ANY)] * 3,
        out_specs=[vmem] * 5,
        scratch_shapes=[
            pltpu.VMEM((3, 3, rows, 128), jnp.float32),
            pltpu.VMEM((3, 2, 8, width), jnp.float32),
            pltpu.SemaphoreType.DMA((3, 3)),
            pltpu.SemaphoreType.DMA((3, 2)),
        ],
        compiler_params=pltpu.CompilerParams(vmem_limit_bytes=56 * 2**20),
        name="strip_edges",
    )(*fields)


def tile_kernel(points_ref, gen_ref, coarse_ref, fine_ref, row_ref, core_ref, own_ref, z_ref, out_ref, inner_ref, kx_ref, ky_ref, v_ref, g_ref, t_ref, s_ref):
    f32 = jnp.float32
    lane = lax.broadcasted_iota(jnp.int32, (1, 128), 1)
    left = lane < SAMPLES
    odd = lax.rem(lax.axis_index("strip"), 2) == 1
    tile = lax.axis_index("samp")
    sines = coarse_ref[0, pl.ds(tile, 1), :] * fine_ref[1] + coarse_ref[1, pl.ds(tile, 1), :] * fine_ref[0]
    high, low = split(sines)
    col_parts = jnp.concatenate([high, low[:, : 2 * MODES]], axis=1)
    row_parts = rows_of_strip(row_ref)

    sample = lax.broadcasted_iota(jnp.int32, (SAMPLES, 128), 0)
    points = jnp.sum(jnp.where(sample == lane % SAMPLES, points_ref[...], 0), axis=0, keepdims=True)
    for p in range(MODES):
        cells = (points * gen_ref[:, p : p + 1]) & 65535
        coords = cells.astype(f32) * (1.0 / 65536.0) - 0.5
        both = jnp.concatenate([jnp.where(left, coords, 0.0), jnp.where(left, 0.0, coords)], axis=0)
        high, low = split(both)
        inner_ref[48 * p : 48 * p + 48, :] = jnp.dot(
            col_parts, jnp.concatenate([high, low, high], axis=0), preferred_element_type=f32
        )

    start_fields = []
    for f in range(3):
        core, far = core_ref[f], z_ref[f]
        x = jnp.concatenate([jnp.where(odd, core, far), own_ref[f], jnp.where(odd, far, core)], axis=0)
        start_fields.append(x * DT if f == 1 else x)
    before = jnp.zeros((TALL, 128), f32)
    for j in range(COLS):
        high, low = split(inner_ref[pl.ds(j, MODES, stride=48), :])
        log = jnp.dot(row_parts, jnp.concatenate([high, low, high], axis=0), preferred_element_type=f32)
        k = 0.5 * DT + (0.5 * DT * 0.8) * jnp.tanh(log)
        kx_ref[j] = before + k
        ky_ref[j] = k + pltpu.roll(k, TALL - 1, 0)
        before = k
        for x, ref in zip(start_fields, (v_ref, g_ref, t_ref)):
            ref[j] = jnp.where(left, x[:, j : j + 1], x[:, j + HALF : j + HALF + 1])

    def divergence(j, carry):
        v, left_flux = carry
        right = v_ref[j + 1]
        right_flux = kx_ref[j + 1] * (right - v)
        down_flux = ky_ref[j] * (pltpu.roll(v, TALL - 1, 0) - v)
        new = v + ((right_flux - left_flux) + (down_flux - pltpu.roll(down_flux, 1, 0)))
        return new, (right, right_flux)

    def sweep(first, body):
        v = v_ref[first]
        start = (v, kx_ref[first] * (v - v_ref[first - 1]))
        return start, first, COLS - first

    def state_step(j, carry):
        new, after = divergence(j, carry)
        v_ref[j] = new + g_ref[j]
        return after

    def last_state_step(j, carry):
        new, after = divergence(j, carry)
        v_ref[j] = new + g_ref[j] - t_ref[j]
        return after

    def first_costate_step(j, carry):
        new, after = divergence(j, carry)
        s_ref[j] = carry[0] + new
        v_ref[j] = new
        return after

    for t, body in enumerate((state_step, state_step, last_state_step, first_costate_step)):
        start, low_j, high_j = sweep(t + 1, body)
        lax.fori_loop(low_j, high_j, body, start, unroll=8)

    source = lax.broadcasted_iota(jnp.int32, (256, 128), 0) % 128 // SAMPLES
    place = lax.broadcasted_iota(jnp.int32, (256, 128), 1) // HALF % 2
    add_samples = (source == place).astype(f32).astype(jnp.bfloat16)

    def last_costate_step(j, carry):
        total, carry = carry
        new, after = divergence(j, carry)
        high, low = split((s_ref[j] + new)[8 : 8 + TILE])
        sums = jnp.dot(jnp.concatenate([high, low], axis=1), add_samples, preferred_element_type=f32)
        return jnp.where(lane % HALF == j - HALO, sums, total), after

    start, low_j, high_j = sweep(HALO, last_costate_step)
    total, _ = lax.fori_loop(low_j, high_j, last_costate_step, (jnp.zeros((TILE, 128), f32), start), unroll=32)

    total = jnp.where(left, total[:HALF], total[HALF:])
    control = own_ref[1]
    top = pltpu.roll(control[:HALF], 128 - HALO, 1)
    bottom = pltpu.roll(control[HALF:], TILE - HALO, 1)
    control = jnp.where(left, top, bottom)
    out_ref[...] = control - RATE * (total * (DT / SAMPLES) + REG * control)


def tile_gradient(*args):
    big = pltpu.VMEM((COLS, TALL, 128), jnp.float32)
    return pl.pallas_call(
        tile_kernel,
        out_shape=jax.ShapeDtypeStruct((HALF, 128), jnp.float32),
        in_specs=[pl.BlockSpec(memory_space=pltpu.VMEM)] * len(args),
        out_specs=pl.BlockSpec(memory_space=pltpu.VMEM),
        scratch_shapes=[pltpu.VMEM((48 * MODES, 128), jnp.float32)] + [big] * 6,
        compiler_params=pltpu.CompilerParams(vmem_limit_bytes=40 * 2**20),
        cost_estimate=pl.CostEstimate(flops=4_000_000_000, bytes_accessed=20_000_000, transcendentals=430_000),
        name="tile_gradient",
    )(*args)


def assemble_kernel(*refs):
    parts, out_ref = refs[:4], refs[4]
    left = lax.broadcasted_iota(jnp.int32, (1, 128), 1) < TILE
    tile = lax.axis_index("samp")
    x, y, z = tile // 16, lax.rem(tile // 4, 4), lax.rem(tile, 4)
    for kx in range(4):
        for pair in range(8):
            to_y, to_z = pair // 2, pair % 2 * 2
            a = parts[kx][y ^ to_y, z ^ to_z]
            b = parts[kx][y ^ to_y, z ^ (to_z + 1)]
            first = pl.multiple_of(((x ^ kx) * 8 + pair) * 128, 128)
            out_ref[:HALF, pl.ds(first, 128)] = jnp.where(left, a, pltpu.roll(b, TILE, 1))
            out_ref[HALF:, pl.ds(first, 128)] = jnp.where(left, pltpu.roll(a, TILE, 1), b)


def assemble(parts):
    return pl.pallas_call(
        assemble_kernel,
        out_shape=jax.ShapeDtypeStruct((TILE, SAMPLES * TILE), jnp.float32),
        in_specs=[pl.BlockSpec(memory_space=pltpu.VMEM)] * 4,
        out_specs=pl.BlockSpec(memory_space=pltpu.VMEM),
        compiler_params=pltpu.CompilerParams(vmem_limit_bytes=16 * 2**20),
        name="assemble",
    )(*parts)


def state_kernel(point_ref, gen_ref, row_ref, coarse_ref, fine_ref, init_ref, control_ref, core_ref, z_ref, out_ref, kx_ref, ky_ref, g_ref, v_ref, w_ref):
    f32 = jnp.float32
    blocks = v_ref.shape[0]
    lane = lax.broadcasted_iota(jnp.int32, (1, 128), 1)
    first, last = lane == 0, lane == 127

    cells = (point_ref[0] * gen_ref[...]) & 65535
    high, low = split(cells.astype(f32) * (1.0 / 65536.0) - 0.5)
    coords = jnp.concatenate([high, high, low], axis=1)

    rows, above = out_ref.shape[0], 8
    row_parts = rows_of_strip(row_ref)
    odd = lax.rem(lax.axis_index("strip"), 2) == 1

    def to_left(value):
        return pltpu.roll(value, 127, 1)

    def up(value):
        return pltpu.roll(value, value.shape[0] - 1, 0)

    before_k, before_shifted, first_shifted = None, None, None
    for b in range(blocks):
        sine = coarse_ref[0][:, b : b + 1] * fine_ref[1] + coarse_ref[1][:, b : b + 1] * fine_ref[0]
        high, low = split(sine)
        inner = jnp.dot(coords, jnp.concatenate([high, low, high], axis=0), preferred_element_type=f32)
        high, low = split(inner)
        log = jnp.dot(row_parts, jnp.concatenate([high, low, high], axis=0), preferred_element_type=f32)
        k = 0.5 * DT + (0.5 * DT * 0.8) * jnp.tanh(log)
        ky_ref[b] = k + up(k)
        shifted = to_left(k)
        if b == 0:
            first_shifted = shifted
        else:
            kx_ref[b - 1] = before_k + jnp.where(last, shifted, before_shifted)
        before_k, before_shifted = k, shifted
        columns = slice(128 * b, 128 * b + 128)
        core, far = core_ref[b], z_ref[b]
        lead, trail = jnp.where(odd, core, far), jnp.where(odd, far, core)
        v_ref[b] = jnp.concatenate([lead, init_ref[:, columns], trail], axis=0)
        g_ref[b] = DT * jnp.concatenate([pltpu.roll(lead, 3, 0), control_ref[:, columns], pltpu.roll(trail, 5, 0)], axis=0)
    kx_ref[blocks - 1] = before_k + jnp.where(last, first_shifted, before_shifted)

    def sweep(source, write):
        v = source[blocks - 1]
        flux = kx_ref[blocks - 1] * (jnp.where(last, to_left(source[0]), to_left(v)) - v)
        start = (source[0], to_left(source[0]), pltpu.roll(flux, 1, 1))

        def step(b, carry):
            v, shifted, flux_before = carry
            following = source[lax.rem(b + 1, blocks)]
            following_shifted = to_left(following)
            flux = kx_ref[b] * (jnp.where(last, following_shifted, shifted) - v)
            flux_shifted = pltpu.roll(flux, 1, 1)
            down = ky_ref[b] * (up(v) - v)
            new = v + ((flux - jnp.where(first, flux_before, flux_shifted)) + (down - pltpu.roll(down, 1, 0)))
            write(b, new + g_ref[b])
            return following, following_shifted, flux_shifted

        lax.fori_loop(0, blocks, step, start, unroll=8)

    def keep(ref):
        def write(b, value):
            ref[b] = value
        return write

    def finish(b, value):
        out_ref[:, pl.ds(pl.multiple_of(b * 128, 128), 128)] = value[above : above + rows]

    sweep(v_ref, keep(w_ref))
    sweep(w_ref, keep(v_ref))
    sweep(v_ref, finish)


def own_final_state(point_index, generator, row_table, initial_state, control, from_core, from_z):
    rows, width = initial_state.shape
    blocks = width // 128
    turns = 2.0 * np.pi / width * RANKS[:, None]
    coarse = turns * (128 * np.arange(blocks))[None, :]
    fine = turns * np.arange(128)[None, :]
    scaled = BY_RANK[:, None]
    coarse = np.stack([np.sin(coarse), np.cos(coarse)]).astype(np.float32)
    fine = np.stack([np.sin(fine) * scaled, np.cos(fine) * scaled]).astype(np.float32)
    big = pltpu.VMEM((blocks, rows + 16, 128), jnp.float32)
    return pl.pallas_call(
        state_kernel,
        out_shape=jax.ShapeDtypeStruct((rows, width), jnp.float32),
        in_specs=[pl.BlockSpec(memory_space=pltpu.SMEM)] + [pl.BlockSpec(memory_space=pltpu.VMEM)] * 8,
        out_specs=pl.BlockSpec(memory_space=pltpu.VMEM),
        scratch_shapes=[big] * 5,
        compiler_params=pltpu.CompilerParams(vmem_limit_bytes=40 * 2**20),
        cost_estimate=pl.CostEstimate(flops=2_000_000_000, bytes_accessed=3_500_000, transcendentals=330_000),
        name="own_final_state",
    )(point_index, generator, row_table, coarse, fine, initial_state, control, from_core, from_z)


CORES = [(s * 4 + k, s * 4 + (k ^ 1)) for s in range(64) for k in range(4)]
ACROSS = [(s * 4 + k, (s ^ 2) * 4 + 3 - k) for s in range(64) for k in range(4)]


def exchange(block, stride):
    others = [lax.ppermute(block, "samp", [(i, i ^ stride * k) for i in range(64)]) for k in (1, 2, 3)]
    return [block] + others


def on_device(initial_state, target, control, point_index, generator):
    rows, width = initial_state.shape
    row_table = row_tables(rows * lax.axis_size("strip"))

    both = ("samp", "strip")
    own, to_core, to_z, wide_to_core, wide_to_z = strip_edges((initial_state, control, target))
    own = jnp.maximum(own, jnp.finfo(jnp.float32).min)
    core, far = lax.ppermute(to_core, both, CORES), lax.ppermute(to_z, both, ACROSS)
    core_wide, far_wide = lax.ppermute(wide_to_core, both, CORES), lax.ppermute(wide_to_z, both, ACROSS)
    points = jnp.broadcast_to(point_index[:, None, None], (SAMPLES, 1, 128))
    points = lax.all_to_all(points, "samp", 0, 0, tiled=True).reshape(SAMPLES, 128)
    mine = tile_gradient(points, generator.T, *tile_col_tables(width), row_table, core, own, far)

    mine, core_wide, far_wide = lax.optimization_barrier((mine, core_wide, far_wide))
    tiles = jnp.stack(exchange(mine, 1))
    tiles = jnp.stack(exchange(tiles, 4))
    tiles, generator = lax.optimization_barrier((tiles, generator))
    new_control = assemble(exchange(tiles, 16))

    state = own_final_state(point_index, generator, row_table, initial_state, control, core_wide, far_wide)
    return (new_control, state[None])


def solution(mesh):
    placed = (P("strip", None), P("strip", None), P("strip", None), P("samp"), P())
    return jax.shard_map(
        on_device,
        mesh=mesh,
        in_specs=placed,
        out_specs=(P("strip", None), P("samp", "strip", None)),
        check_vma=False,
    )
```

```python
import jax
import jax.numpy as jnp
import numpy as np
from jax import lax
from jax.experimental import pallas as pl
from jax.experimental.pallas import tpu as pltpu
from jax.sharding import PartitionSpec as P

STEPS = 3
DT = 0.12
REG = 0.1
RATE = 1.0
SAMPLES = 64
MODES = 32
HALO = 2 * STEPS - 1
TILE = 64
HALF = TILE // 2
COLS = HALF + 2 * HALO
TALL = TILE + 16

RANKS = np.arange(1, MODES + 1)
BY_RANK = (1.0 / np.sqrt(RANKS)).astype(np.float32)
SCALE = np.float32(4.0 / np.sum(1.0 / RANKS))


def split(value):
    high = value.astype(jnp.bfloat16)
    return high, (value - high.astype(jnp.float32)).astype(jnp.bfloat16)


def both_parts(value):
    high = value.astype(jnp.bfloat16)
    low = (value - high.astype(np.float32)).astype(jnp.bfloat16)
    return np.concatenate([high, high, low], axis=1)


def row_tables(grid_rows):
    places = np.arange(-8, grid_rows + 8)[:, None]
    sines = np.sin(2.0 * np.pi * (places * RANKS[None, :] % grid_rows) / grid_rows)
    return both_parts((sines * BY_RANK * SCALE).astype(np.float32))


def rows_of_strip(row_ref):
    first = pl.multiple_of(lax.axis_index("strip") * TILE, TILE)
    return row_ref[pl.ds(first, TALL), :]


def tile_col_tables(width):
    ranks = np.tile(RANKS, 4)[None, :]
    turn = 2.0 * np.pi / width
    coarse = turn * (TILE * np.arange(width // TILE)[:, None] * ranks % width)
    half = np.repeat([0, HALF, 0, HALF], MODES)[None, :]
    fine = turn * ((np.arange(48)[:, None] - HALO + half) * ranks % width)
    scaled = np.tile(BY_RANK, 4)[None, :]
    coarse = np.stack([np.sin(coarse), np.cos(coarse)])
    fine = np.stack([np.sin(fine) * scaled, np.cos(fine) * scaled])
    return coarse.astype(np.float32), fine.astype(np.float32)


def window_of(parts, tile):
    line = jnp.concatenate(parts, axis=1)
    even_part = line[:, 128 - HALO : 256 - HALO]
    odd_part = line[:, 192 - HALO : 320 - HALO]
    return jnp.where(lax.rem(tile, 2) == 1, odd_part, even_part)


def edge_rows(rows):
    odd = lax.rem(lax.axis_index("strip"), 2)
    return pl.multiple_of((1 - odd) * (rows - 8), 8), pl.multiple_of(odd * (rows - 8), 8)


def edges_kernel(*refs):
    fields, (own, to_core, to_z, wide_to_core, wide_to_z), near, edge, sems, edge_sems = refs[:3], refs[3:8], *refs[8:]
    rows, width = fields[0].shape
    blocks = width // 128
    tile = lax.axis_index("samp")
    firsts = edge_rows(rows)

    def column_block(t, n):
        block = lax.rem(t // 2 + (blocks - 1 + n), blocks)
        return pl.ds(pl.multiple_of(block * 128, 128), 128)

    copies = []
    for n in range(2):
        for f in range(3):
            copies.append(pltpu.make_async_copy(fields[f].at[pl.ds(firsts[n], 8), :], edge.at[f, n], edge_sems.at[f, n]))
    for f in range(3):
        for n in range(3):
            copies.append(pltpu.make_async_copy(fields[f].at[:, column_block(tile, n)], near.at[f, n], sems.at[f, n]))
    for copy in copies:
        copy.start()
    for copy in copies:
        copy.wait()

    odd = lax.rem(lax.axis_index("strip"), 2)
    for f in range(3):
        own[f] = window_of([near[f, n] for n in range(3)], tile)
        for n, (out, partner) in enumerate(((to_core, tile), (to_z, tile ^ 2))):
            out[f] = window_of([edge[f, n, :, column_block(partner, m)] for m in range(3)], tile)
    row = lax.broadcasted_iota(jnp.int32, (8, 128), 0)
    for n, out in enumerate((wide_to_core, wide_to_z)):
        is_tail = odd == n
        is_state = jnp.where(is_tail, row, 7 - row) >= 8 - STEPS
        for b in range(blocks):
            columns = slice(128 * b, 128 * b + 128)
            source = edge[1, n, :, columns]
            moved = jnp.where(is_tail, pltpu.roll(source, 5, 0), pltpu.roll(source, 3, 0))
            out[b] = jnp.where(is_state, edge[0, n, :, columns], moved)


def strip_edges(fields):
    rows, width = fields[0].shape
    vmem = pl.BlockSpec(memory_space=pltpu.VMEM)
    shapes = [(3, rows, 128), (3, 8, 128), (3, 8, 128), (width // 128, 8, 128), (width // 128, 8, 128)]
    return pl.pallas_call(
        edges_kernel,
        out_shape=[jax.ShapeDtypeStruct(shape, jnp.float32) for shape in shapes],
        in_specs=[pl.BlockSpec(memory_space=pl.ANY)] * 3,
        out_specs=[vmem] * 5,
        scratch_shapes=[
            pltpu.VMEM((3, 3, rows, 128), jnp.float32),
            pltpu.VMEM((3, 2, 8, width), jnp.float32),
            pltpu.SemaphoreType.DMA((3, 3)),
            pltpu.SemaphoreType.DMA((3, 2)),
        ],
        compiler_params=pltpu.CompilerParams(vmem_limit_bytes=56 * 2**20),
        name="strip_edges",
    )(*fields)


def tile_kernel(points_ref, gen_ref, coarse_ref, fine_ref, row_ref, core_ref, own_ref, z_ref, out_ref, inner_ref, kx_ref, ky_ref, v_ref, g_ref, t_ref, s_ref):
    f32 = jnp.float32
    lane = lax.broadcasted_iota(jnp.int32, (1, 128), 1)
    left = lane < SAMPLES
    odd = lax.rem(lax.axis_index("strip"), 2) == 1
    tile = lax.axis_index("samp")
    sines = coarse_ref[0, pl.ds(tile, 1), :] * fine_ref[1] + coarse_ref[1, pl.ds(tile, 1), :] * fine_ref[0]
    high, low = split(sines)
    col_parts = jnp.concatenate([high, low[:, : 2 * MODES]], axis=1)
    row_parts = rows_of_strip(row_ref)

    sample = lax.broadcasted_iota(jnp.int32, (SAMPLES, 128), 0)
    points = jnp.sum(jnp.where(sample == lane % SAMPLES, points_ref[...], 0), axis=0, keepdims=True)
    for p in range(MODES):
        cells = (points * gen_ref[:, p : p + 1]) & 65535
        coords = cells.astype(f32) * (1.0 / 65536.0) - 0.5
        both = jnp.concatenate([jnp.where(left, coords, 0.0), jnp.where(left, 0.0, coords)], axis=0)
        high, low = split(both)
        inner_ref[48 * p : 48 * p + 48, :] = jnp.dot(
            col_parts, jnp.concatenate([high, low, high], axis=0), preferred_element_type=f32
        )

    start_fields = []
    for f in range(3):
        core, far = core_ref[f], z_ref[f]
        x = jnp.concatenate([jnp.where(odd, core, far), own_ref[f], jnp.where(odd, far, core)], axis=0)
        start_fields.append(x * DT if f == 1 else x)
    before = jnp.zeros((TALL, 128), f32)
    for j in range(COLS):
        high, low = split(inner_ref[pl.ds(j, MODES, stride=48), :])
        log = jnp.dot(row_parts, jnp.concatenate([high, low, high], axis=0), preferred_element_type=f32)
        k = 0.5 * DT + (0.5 * DT * 0.8) * jnp.tanh(log)
        kx_ref[j] = before + k
        ky_ref[j] = k + pltpu.roll(k, TALL - 1, 0)
        before = k
        for x, ref in zip(start_fields, (v_ref, g_ref, t_ref)):
            ref[j] = jnp.where(left, x[:, j : j + 1], x[:, j + HALF : j + HALF + 1])

    def divergence(j, carry):
        v, left_flux = carry
        right = v_ref[j + 1]
        right_flux = kx_ref[j + 1] * (right - v)
        down_flux = ky_ref[j] * (pltpu.roll(v, TALL - 1, 0) - v)
        new = v + ((right_flux - left_flux) + (down_flux - pltpu.roll(down_flux, 1, 0)))
        return new, (right, right_flux)

    def sweep(first, body):
        v = v_ref[first]
        start = (v, kx_ref[first] * (v - v_ref[first - 1]))
        return start, first, COLS - first

    def state_step(j, carry):
        new, after = divergence(j, carry)
        v_ref[j] = new + g_ref[j]
        return after

    def last_state_step(j, carry):
        new, after = divergence(j, carry)
        v_ref[j] = new + g_ref[j] - t_ref[j]
        return after

    def first_costate_step(j, carry):
        new, after = divergence(j, carry)
        s_ref[j] = carry[0] + new
        v_ref[j] = new
        return after

    for t, body in enumerate((state_step, state_step, last_state_step, first_costate_step)):
        start, low_j, high_j = sweep(t + 1, body)
        lax.fori_loop(low_j, high_j, body, start, unroll=8)

    source = lax.broadcasted_iota(jnp.int32, (256, 128), 0) % 128 // SAMPLES
    place = lax.broadcasted_iota(jnp.int32, (256, 128), 1) // HALF % 2
    add_samples = (source == place).astype(f32).astype(jnp.bfloat16)

    def last_costate_step(j, carry):
        total, carry = carry
        new, after = divergence(j, carry)
        high, low = split((s_ref[j] + new)[8 : 8 + TILE])
        sums = jnp.dot(jnp.concatenate([high, low], axis=1), add_samples, preferred_element_type=f32)
        return jnp.where(lane % HALF == j - HALO, sums, total), after

    start, low_j, high_j = sweep(HALO, last_costate_step)
    total, _ = lax.fori_loop(low_j, high_j, last_costate_step, (jnp.zeros((TILE, 128), f32), start), unroll=32)

    total = jnp.where(left, total[:HALF], total[HALF:])
    control = own_ref[1]
    top = pltpu.roll(control[:HALF], 128 - HALO, 1)
    bottom = pltpu.roll(control[HALF:], TILE - HALO, 1)
    control = jnp.where(left, top, bottom)
    out_ref[...] = control - RATE * (total * (DT / SAMPLES) + REG * control)


def tile_gradient(*args):
    big = pltpu.VMEM((COLS, TALL, 128), jnp.float32)
    return pl.pallas_call(
        tile_kernel,
        out_shape=jax.ShapeDtypeStruct((HALF, 128), jnp.float32),
        in_specs=[pl.BlockSpec(memory_space=pltpu.VMEM)] * len(args),
        out_specs=pl.BlockSpec(memory_space=pltpu.VMEM),
        scratch_shapes=[pltpu.VMEM((48 * MODES, 128), jnp.float32)] + [big] * 6,
        compiler_params=pltpu.CompilerParams(vmem_limit_bytes=40 * 2**20),
        cost_estimate=pl.CostEstimate(flops=4_000_000_000, bytes_accessed=20_000_000, transcendentals=430_000),
        name="tile_gradient",
    )(*args)


def assemble_kernel(*refs):
    parts, out_ref = refs[:4], refs[4]
    left = lax.broadcasted_iota(jnp.int32, (1, 128), 1) < TILE
    tile = lax.axis_index("samp")
    x, y, z = tile // 16, lax.rem(tile // 4, 4), lax.rem(tile, 4)
    for kx in range(4):
        for pair in range(8):
            to_y, to_z = pair // 2, pair % 2 * 2
            a = parts[kx][y ^ to_y, z ^ to_z]
            b = parts[kx][y ^ to_y, z ^ (to_z + 1)]
            first = pl.multiple_of(((x ^ kx) * 8 + pair) * 128, 128)
            out_ref[:HALF, pl.ds(first, 128)] = jnp.where(left, a, pltpu.roll(b, TILE, 1))
            out_ref[HALF:, pl.ds(first, 128)] = jnp.where(left, pltpu.roll(a, TILE, 1), b)


def assemble(parts):
    return pl.pallas_call(
        assemble_kernel,
        out_shape=jax.ShapeDtypeStruct((TILE, SAMPLES * TILE), jnp.float32),
        in_specs=[pl.BlockSpec(memory_space=pltpu.VMEM)] * 4,
        out_specs=pl.BlockSpec(memory_space=pltpu.VMEM),
        compiler_params=pltpu.CompilerParams(vmem_limit_bytes=16 * 2**20),
        name="assemble",
    )(*parts)


def state_kernel(point_ref, gen_ref, row_ref, coarse_ref, fine_ref, init_ref, control_ref, core_ref, z_ref, out_ref, kx_ref, ky_ref, g_ref, v_ref, w_ref):
    f32 = jnp.float32
    blocks = v_ref.shape[0]
    lane = lax.broadcasted_iota(jnp.int32, (1, 128), 1)
    first, last = lane == 0, lane == 127

    cells = (point_ref[0] * gen_ref[...]) & 65535
    high, low = split(cells.astype(f32) * (1.0 / 65536.0) - 0.5)
    coords = jnp.concatenate([high, high, low], axis=1)

    rows, above = out_ref.shape[0], 8
    row_parts = rows_of_strip(row_ref)
    odd = lax.rem(lax.axis_index("strip"), 2) == 1

    def to_left(value):
        return pltpu.roll(value, 127, 1)

    def up(value):
        return pltpu.roll(value, value.shape[0] - 1, 0)

    before_k, before_shifted, first_shifted = None, None, None
    for b in range(blocks):
        sine = coarse_ref[0][:, b : b + 1] * fine_ref[1] + coarse_ref[1][:, b : b + 1] * fine_ref[0]
        high, low = split(sine)
        inner = jnp.dot(coords, jnp.concatenate([high, low, high], axis=0), preferred_element_type=f32)
        high, low = split(inner)
        log = jnp.dot(row_parts, jnp.concatenate([high, low, high], axis=0), preferred_element_type=f32)
        k = 0.5 * DT + (0.5 * DT * 0.8) * jnp.tanh(log)
        ky_ref[b] = k + up(k)
        shifted = to_left(k)
        if b == 0:
            first_shifted = shifted
        else:
            kx_ref[b - 1] = before_k + jnp.where(last, shifted, before_shifted)
        before_k, before_shifted = k, shifted
        columns = slice(128 * b, 128 * b + 128)
        core, far = core_ref[b], z_ref[b]
        lead, trail = jnp.where(odd, core, far), jnp.where(odd, far, core)
        v_ref[b] = jnp.concatenate([lead, init_ref[:, columns], trail], axis=0)
        g_ref[b] = DT * jnp.concatenate([pltpu.roll(lead, 3, 0), control_ref[:, columns], pltpu.roll(trail, 5, 0)], axis=0)
    kx_ref[blocks - 1] = before_k + jnp.where(last, first_shifted, before_shifted)

    def sweep(source, write):
        v = source[blocks - 1]
        flux = kx_ref[blocks - 1] * (jnp.where(last, to_left(source[0]), to_left(v)) - v)
        start = (source[0], to_left(source[0]), pltpu.roll(flux, 1, 1))

        def step(b, carry):
            v, shifted, flux_before = carry
            following = source[lax.rem(b + 1, blocks)]
            following_shifted = to_left(following)
            flux = kx_ref[b] * (jnp.where(last, following_shifted, shifted) - v)
            flux_shifted = pltpu.roll(flux, 1, 1)
            down = ky_ref[b] * (up(v) - v)
            new = v + ((flux - jnp.where(first, flux_before, flux_shifted)) + (down - pltpu.roll(down, 1, 0)))
            write(b, new + g_ref[b])
            return following, following_shifted, flux_shifted

        lax.fori_loop(0, blocks, step, start, unroll=8)

    def keep(ref):
        def write(b, value):
            ref[b] = value
        return write

    def finish(b, value):
        out_ref[:, pl.ds(pl.multiple_of(b * 128, 128), 128)] = value[above : above + rows]

    sweep(v_ref, keep(w_ref))
    sweep(w_ref, keep(v_ref))
    sweep(v_ref, finish)


def own_final_state(point_index, generator, row_table, initial_state, control, from_core, from_z):
    rows, width = initial_state.shape
    blocks = width // 128
    turns = 2.0 * np.pi / width * RANKS[:, None]
    coarse = turns * (128 * np.arange(blocks))[None, :]
    fine = turns * np.arange(128)[None, :]
    scaled = BY_RANK[:, None]
    coarse = np.stack([np.sin(coarse), np.cos(coarse)]).astype(np.float32)
    fine = np.stack([np.sin(fine) * scaled, np.cos(fine) * scaled]).astype(np.float32)
    big = pltpu.VMEM((blocks, rows + 16, 128), jnp.float32)
    return pl.pallas_call(
        state_kernel,
        out_shape=jax.ShapeDtypeStruct((rows, width), jnp.float32),
        in_specs=[pl.BlockSpec(memory_space=pltpu.SMEM)] + [pl.BlockSpec(memory_space=pltpu.VMEM)] * 8,
        out_specs=pl.BlockSpec(memory_space=pltpu.VMEM),
        scratch_shapes=[big] * 5,
        compiler_params=pltpu.CompilerParams(vmem_limit_bytes=40 * 2**20),
        cost_estimate=pl.CostEstimate(flops=2_000_000_000, bytes_accessed=3_500_000, transcendentals=330_000),
        name="own_final_state",
    )(point_index, generator, row_table, coarse, fine, initial_state, control, from_core, from_z)


CORES = [(s * 4 + k, s * 4 + (k ^ 1)) for s in range(64) for k in range(4)]
ACROSS = [(s * 4 + k, (s ^ 2) * 4 + 3 - k) for s in range(64) for k in range(4)]


def exchange(block, stride):
    others = [lax.ppermute(block, "samp", [(i, i ^ stride * k) for i in range(64)]) for k in (1, 2, 3)]
    return [block] + others


def on_device(initial_state, target, control, point_index, generator):
    rows, width = initial_state.shape
    row_table = row_tables(rows * lax.axis_size("strip"))

    both = ("samp", "strip")
    own, to_core, to_z, wide_to_core, wide_to_z = strip_edges((initial_state, control, target))
    own = jnp.maximum(own, jnp.finfo(jnp.float32).min)
    core, far = lax.ppermute(to_core, both, CORES), lax.ppermute(to_z, both, ACROSS)
    core_wide, far_wide = lax.ppermute(wide_to_core, both, CORES), lax.ppermute(wide_to_z, both, ACROSS)
    points = jnp.broadcast_to(point_index[:, None, None], (SAMPLES, 1, 128))
    points = lax.all_to_all(points, "samp", 0, 0, tiled=True).reshape(SAMPLES, 128)
    mine = tile_gradient(points, generator.T, *tile_col_tables(width), row_table, core, own, far)

    tiles = jnp.stack(exchange(mine, 1))
    tiles, core_wide, far_wide = lax.optimization_barrier((tiles, core_wide, far_wide))
    tiles = jnp.stack(exchange(tiles, 4))
    tiles, generator = lax.optimization_barrier((tiles, generator))
    new_control = assemble(exchange(tiles, 16))

    state = own_final_state(point_index, generator, row_table, initial_state, control, core_wide, far_wide)
    return (new_control, state[None])


def solution(mesh):
    placed = (P("strip", None), P("strip", None), P("strip", None), P("samp"), P())
    return jax.shard_map(
        on_device,
        mesh=mesh,
        in_specs=placed,
        out_specs=(P("strip", None), P("samp", "strip", None)),
        check_vma=False,
    )
```

```python
import jax
import jax.numpy as jnp
import numpy as np
from jax import lax
from jax.experimental import pallas as pl
from jax.experimental.pallas import tpu as pltpu
from jax.sharding import PartitionSpec as P

STEPS = 3
DT = 0.12
REG = 0.1
RATE = 1.0
SAMPLES = 64
MODES = 32
HALO = 2 * STEPS - 1
TILE = 64
HALF = TILE // 2
COLS = HALF + 2 * HALO
TALL = TILE + 16

RANKS = np.arange(1, MODES + 1)
BY_RANK = (1.0 / np.sqrt(RANKS)).astype(np.float32)
SCALE = np.float32(4.0 / np.sum(1.0 / RANKS))


def split(value):
    high = value.astype(jnp.bfloat16)
    return high, (value - high.astype(jnp.float32)).astype(jnp.bfloat16)


def both_parts(value):
    high = value.astype(jnp.bfloat16)
    low = (value - high.astype(np.float32)).astype(jnp.bfloat16)
    return np.concatenate([high, high, low], axis=1)


def row_tables(grid_rows):
    places = np.arange(-8, grid_rows + 8)[:, None]
    sines = np.sin(2.0 * np.pi * (places * RANKS[None, :] % grid_rows) / grid_rows)
    return both_parts((sines * BY_RANK * SCALE).astype(np.float32))


def rows_of_strip(row_ref):
    first = pl.multiple_of(lax.axis_index("strip") * TILE, TILE)
    return row_ref[pl.ds(first, TALL), :]


def tile_col_tables(width):
    ranks = np.tile(RANKS, 4)[None, :]
    turn = 2.0 * np.pi / width
    coarse = turn * (TILE * np.arange(width // TILE)[:, None] * ranks % width)
    half = np.repeat([0, HALF, 0, HALF], MODES)[None, :]
    fine = turn * ((np.arange(48)[:, None] - HALO + half) * ranks % width)
    scaled = np.tile(BY_RANK, 4)[None, :]
    coarse = np.stack([np.sin(coarse), np.cos(coarse)])
    fine = np.stack([np.sin(fine) * scaled, np.cos(fine) * scaled])
    return coarse.astype(np.float32), fine.astype(np.float32)


def window_of(parts, tile):
    line = jnp.concatenate(parts, axis=1)
    even_part = line[:, 128 - HALO : 256 - HALO]
    odd_part = line[:, 192 - HALO : 320 - HALO]
    return jnp.where(lax.rem(tile, 2) == 1, odd_part, even_part)


def edge_rows(rows):
    odd = lax.rem(lax.axis_index("strip"), 2)
    return pl.multiple_of((1 - odd) * (rows - 8), 8), pl.multiple_of(odd * (rows - 8), 8)


def edges_kernel(*refs):
    fields, (own, to_core, to_z, wide_to_core, wide_to_z), near, edge, sems, edge_sems = refs[:3], refs[3:8], *refs[8:]
    rows, width = fields[0].shape
    blocks = width // 128
    tile = lax.axis_index("samp")
    firsts = edge_rows(rows)

    def column_block(t, n):
        block = lax.rem(t // 2 + (blocks - 1 + n), blocks)
        return pl.ds(pl.multiple_of(block * 128, 128), 128)

    copies = []
    for n in range(2):
        for f in range(3):
            copies.append(pltpu.make_async_copy(fields[f].at[pl.ds(firsts[n], 8), :], edge.at[f, n], edge_sems.at[f, n]))
    for f in range(3):
        for n in range(3):
            copies.append(pltpu.make_async_copy(fields[f].at[:, column_block(tile, n)], near.at[f, n], sems.at[f, n]))
    for copy in copies:
        copy.start()
    for copy in copies:
        copy.wait()

    odd = lax.rem(lax.axis_index("strip"), 2)
    for f in range(3):
        own[f] = window_of([near[f, n] for n in range(3)], tile)
        for n, (out, partner) in enumerate(((to_core, tile), (to_z, tile ^ 2))):
            out[f] = window_of([edge[f, n, :, column_block(partner, m)] for m in range(3)], tile)
    row = lax.broadcasted_iota(jnp.int32, (8, 128), 0)
    for n, out in enumerate((wide_to_core, wide_to_z)):
        is_tail = odd == n
        is_state = jnp.where(is_tail, row, 7 - row) >= 8 - STEPS
        for b in range(blocks):
            columns = slice(128 * b, 128 * b + 128)
            source = edge[1, n, :, columns]
            moved = jnp.where(is_tail, pltpu.roll(source, 5, 0), pltpu.roll(source, 3, 0))
            out[b] = jnp.where(is_state, edge[0, n, :, columns], moved)


def strip_edges(fields):
    rows, width = fields[0].shape
    vmem = pl.BlockSpec(memory_space=pltpu.VMEM)
    shapes = [(3, rows, 128), (3, 8, 128), (3, 8, 128), (width // 128, 8, 128), (width // 128, 8, 128)]
    return pl.pallas_call(
        edges_kernel,
        out_shape=[jax.ShapeDtypeStruct(shape, jnp.float32) for shape in shapes],
        in_specs=[pl.BlockSpec(memory_space=pl.ANY)] * 3,
        out_specs=[vmem] * 5,
        scratch_shapes=[
            pltpu.VMEM((3, 3, rows, 128), jnp.float32),
            pltpu.VMEM((3, 2, 8, width), jnp.float32),
            pltpu.SemaphoreType.DMA((3, 3)),
            pltpu.SemaphoreType.DMA((3, 2)),
        ],
        compiler_params=pltpu.CompilerParams(vmem_limit_bytes=56 * 2**20),
        name="strip_edges",
    )(*fields)


def tile_kernel(points_ref, gen_ref, coarse_ref, fine_ref, row_ref, core_ref, own_ref, z_ref, out_ref, inner_ref, kx_ref, ky_ref, v_ref, g_ref, t_ref, s_ref):
    f32 = jnp.float32
    lane = lax.broadcasted_iota(jnp.int32, (1, 128), 1)
    left = lane < SAMPLES
    odd = lax.rem(lax.axis_index("strip"), 2) == 1
    tile = lax.axis_index("samp")
    sines = coarse_ref[0, pl.ds(tile, 1), :] * fine_ref[1] + coarse_ref[1, pl.ds(tile, 1), :] * fine_ref[0]
    high, low = split(sines)
    col_parts = jnp.concatenate([high, low[:, : 2 * MODES]], axis=1)
    row_parts = rows_of_strip(row_ref)

    sample = lax.broadcasted_iota(jnp.int32, (SAMPLES, 128), 0)
    points = jnp.sum(jnp.where(sample == lane % SAMPLES, points_ref[...], 0), axis=0, keepdims=True)
    for p in range(MODES):
        cells = (points * gen_ref[:, p : p + 1]) & 65535
        coords = cells.astype(f32) * (1.0 / 65536.0) - 0.5
        both = jnp.concatenate([jnp.where(left, coords, 0.0), jnp.where(left, 0.0, coords)], axis=0)
        high, low = split(both)
        inner_ref[48 * p : 48 * p + 48, :] = jnp.dot(
            col_parts, jnp.concatenate([high, low, high], axis=0), preferred_element_type=f32
        )

    start_fields = []
    for f in range(3):
        core, far = core_ref[f], z_ref[f]
        x = jnp.concatenate([jnp.where(odd, core, far), own_ref[f], jnp.where(odd, far, core)], axis=0)
        start_fields.append(x * DT if f == 1 else x)
    before = jnp.zeros((TALL, 128), f32)
    for j in range(COLS):
        high, low = split(inner_ref[pl.ds(j, MODES, stride=48), :])
        log = jnp.dot(row_parts, jnp.concatenate([high, low, high], axis=0), preferred_element_type=f32)
        k = 0.5 * DT + (0.5 * DT * 0.8) * jnp.tanh(log)
        kx_ref[j] = before + k
        ky_ref[j] = k + pltpu.roll(k, TALL - 1, 0)
        before = k
        for x, ref in zip(start_fields, (v_ref, g_ref, t_ref)):
            ref[j] = jnp.where(left, x[:, j : j + 1], x[:, j + HALF : j + HALF + 1])

    def divergence(j, carry):
        v, left_flux = carry
        right = v_ref[j + 1]
        right_flux = kx_ref[j + 1] * (right - v)
        down_flux = ky_ref[j] * (pltpu.roll(v, TALL - 1, 0) - v)
        new = v + ((right_flux - left_flux) + (down_flux - pltpu.roll(down_flux, 1, 0)))
        return new, (right, right_flux)

    def sweep(first, body):
        v = v_ref[first]
        start = (v, kx_ref[first] * (v - v_ref[first - 1]))
        return start, first, COLS - first

    def state_step(j, carry):
        new, after = divergence(j, carry)
        v_ref[j] = new + g_ref[j]
        return after

    def last_state_step(j, carry):
        new, after = divergence(j, carry)
        v_ref[j] = new + g_ref[j] - t_ref[j]
        return after

    def first_costate_step(j, carry):
        new, after = divergence(j, carry)
        s_ref[j] = carry[0] + new
        v_ref[j] = new
        return after

    for t, body in enumerate((state_step, state_step, last_state_step, first_costate_step)):
        start, low_j, high_j = sweep(t + 1, body)
        lax.fori_loop(low_j, high_j, body, start, unroll=8)

    source = lax.broadcasted_iota(jnp.int32, (256, 128), 0) % 128 // SAMPLES
    place = lax.broadcasted_iota(jnp.int32, (256, 128), 1) // HALF % 2
    add_samples = (source == place).astype(f32).astype(jnp.bfloat16)

    def last_costate_step(j, carry):
        total, carry = carry
        new, after = divergence(j, carry)
        high, low = split((s_ref[j] + new)[8 : 8 + TILE])
        sums = jnp.dot(jnp.concatenate([high, low], axis=1), add_samples, preferred_element_type=f32)
        return jnp.where(lane % HALF == j - HALO, sums, total), after

    start, low_j, high_j = sweep(HALO, last_costate_step)
    total, _ = lax.fori_loop(low_j, high_j, last_costate_step, (jnp.zeros((TILE, 128), f32), start), unroll=32)

    total = jnp.where(left, total[:HALF], total[HALF:])
    control = own_ref[1]
    top = pltpu.roll(control[:HALF], 128 - HALO, 1)
    bottom = pltpu.roll(control[HALF:], TILE - HALO, 1)
    control = jnp.where(left, top, bottom)
    out_ref[...] = control - RATE * (total * (DT / SAMPLES) + REG * control)


def tile_gradient(*args):
    big = pltpu.VMEM((COLS, TALL, 128), jnp.float32)
    return pl.pallas_call(
        tile_kernel,
        out_shape=jax.ShapeDtypeStruct((HALF, 128), jnp.float32),
        in_specs=[pl.BlockSpec(memory_space=pltpu.VMEM)] * len(args),
        out_specs=pl.BlockSpec(memory_space=pltpu.VMEM),
        scratch_shapes=[pltpu.VMEM((48 * MODES, 128), jnp.float32)] + [big] * 6,
        compiler_params=pltpu.CompilerParams(vmem_limit_bytes=40 * 2**20),
        cost_estimate=pl.CostEstimate(flops=4_000_000_000, bytes_accessed=20_000_000, transcendentals=430_000),
        name="tile_gradient",
    )(*args)


def assemble_kernel(*refs):
    parts, out_ref = refs[:4], refs[4]
    left = lax.broadcasted_iota(jnp.int32, (1, 128), 1) < TILE
    tile = lax.axis_index("samp")
    x, y, z = tile // 16, lax.rem(tile // 4, 4), lax.rem(tile, 4)
    for ky in range(4):
        for pair in range(8):
            to_x, to_z = pair // 2, pair % 2 * 2
            a = parts[ky][x ^ to_x, z ^ to_z]
            b = parts[ky][x ^ to_x, z ^ (to_z + 1)]
            first = pl.multiple_of((to_x * 8 + (y ^ ky) * 2 + to_z // 2) * 128, 128)
            out_ref[:HALF, pl.ds(first, 128)] = jnp.where(left, a, pltpu.roll(b, TILE, 1))
            out_ref[HALF:, pl.ds(first, 128)] = jnp.where(left, pltpu.roll(a, TILE, 1), b)


def assemble(parts):
    return pl.pallas_call(
        assemble_kernel,
        out_shape=jax.ShapeDtypeStruct((TILE, SAMPLES * TILE), jnp.float32),
        in_specs=[pl.BlockSpec(memory_space=pltpu.VMEM)] * 4,
        out_specs=pl.BlockSpec(memory_space=pltpu.VMEM),
        compiler_params=pltpu.CompilerParams(vmem_limit_bytes=16 * 2**20),
        name="assemble",
    )(*parts)


def state_kernel(point_ref, gen_ref, row_ref, coarse_ref, fine_ref, init_ref, control_ref, core_ref, z_ref, out_ref, kx_ref, ky_ref, g_ref, v_ref, w_ref):
    f32 = jnp.float32
    blocks = v_ref.shape[0]
    lane = lax.broadcasted_iota(jnp.int32, (1, 128), 1)
    first, last = lane == 0, lane == 127

    cells = (point_ref[0] * gen_ref[...]) & 65535
    high, low = split(cells.astype(f32) * (1.0 / 65536.0) - 0.5)
    coords = jnp.concatenate([high, high, low], axis=1)

    rows, above = out_ref.shape[0], 8
    row_parts = rows_of_strip(row_ref)
    odd = lax.rem(lax.axis_index("strip"), 2) == 1

    def to_left(value):
        return pltpu.roll(value, 127, 1)

    def up(value):
        return pltpu.roll(value, value.shape[0] - 1, 0)

    before_k, before_shifted, first_shifted = None, None, None
    for b in range(blocks):
        sine = coarse_ref[0][:, b : b + 1] * fine_ref[1] + coarse_ref[1][:, b : b + 1] * fine_ref[0]
        high, low = split(sine)
        inner = jnp.dot(coords, jnp.concatenate([high, low, high], axis=0), preferred_element_type=f32)
        high, low = split(inner)
        log = jnp.dot(row_parts, jnp.concatenate([high, low, high], axis=0), preferred_element_type=f32)
        k = 0.5 * DT + (0.5 * DT * 0.8) * jnp.tanh(log)
        ky_ref[b] = k + up(k)
        shifted = to_left(k)
        if b == 0:
            first_shifted = shifted
        else:
            kx_ref[b - 1] = before_k + jnp.where(last, shifted, before_shifted)
        before_k, before_shifted = k, shifted
        columns = slice(128 * b, 128 * b + 128)
        core, far = core_ref[b], z_ref[b]
        lead, trail = jnp.where(odd, core, far), jnp.where(odd, far, core)
        v_ref[b] = jnp.concatenate([lead, init_ref[:, columns], trail], axis=0)
        g_ref[b] = DT * jnp.concatenate([pltpu.roll(lead, 3, 0), control_ref[:, columns], pltpu.roll(trail, 5, 0)], axis=0)
    kx_ref[blocks - 1] = before_k + jnp.where(last, first_shifted, before_shifted)

    def sweep(source, write):
        v = source[blocks - 1]
        flux = kx_ref[blocks - 1] * (jnp.where(last, to_left(source[0]), to_left(v)) - v)
        start = (source[0], to_left(source[0]), pltpu.roll(flux, 1, 1))

        def step(b, carry):
            v, shifted, flux_before = carry
            following = source[lax.rem(b + 1, blocks)]
            following_shifted = to_left(following)
            flux = kx_ref[b] * (jnp.where(last, following_shifted, shifted) - v)
            flux_shifted = pltpu.roll(flux, 1, 1)
            down = ky_ref[b] * (up(v) - v)
            new = v + ((flux - jnp.where(first, flux_before, flux_shifted)) + (down - pltpu.roll(down, 1, 0)))
            write(b, new + g_ref[b])
            return following, following_shifted, flux_shifted

        lax.fori_loop(0, blocks, step, start, unroll=8)

    def keep(ref):
        def write(b, value):
            ref[b] = value
        return write

    def finish(b, value):
        out_ref[:, pl.ds(pl.multiple_of(b * 128, 128), 128)] = value[above : above + rows]

    sweep(v_ref, keep(w_ref))
    sweep(w_ref, keep(v_ref))
    sweep(v_ref, finish)


def own_final_state(point_index, generator, row_table, initial_state, control, from_core, from_z):
    rows, width = initial_state.shape
    blocks = width // 128
    turns = 2.0 * np.pi / width * RANKS[:, None]
    coarse = turns * (128 * np.arange(blocks))[None, :]
    fine = turns * np.arange(128)[None, :]
    scaled = BY_RANK[:, None]
    coarse = np.stack([np.sin(coarse), np.cos(coarse)]).astype(np.float32)
    fine = np.stack([np.sin(fine) * scaled, np.cos(fine) * scaled]).astype(np.float32)
    big = pltpu.VMEM((blocks, rows + 16, 128), jnp.float32)
    return pl.pallas_call(
        state_kernel,
        out_shape=jax.ShapeDtypeStruct((rows, width), jnp.float32),
        in_specs=[pl.BlockSpec(memory_space=pltpu.SMEM)] + [pl.BlockSpec(memory_space=pltpu.VMEM)] * 8,
        out_specs=pl.BlockSpec(memory_space=pltpu.VMEM),
        scratch_shapes=[big] * 5,
        compiler_params=pltpu.CompilerParams(vmem_limit_bytes=40 * 2**20),
        cost_estimate=pl.CostEstimate(flops=2_000_000_000, bytes_accessed=3_500_000, transcendentals=330_000),
        name="own_final_state",
    )(point_index, generator, row_table, coarse, fine, initial_state, control, from_core, from_z)


CORES = [(s * 4 + k, s * 4 + (k ^ 1)) for s in range(64) for k in range(4)]
ACROSS = [(s * 4 + k, (s ^ 2) * 4 + 3 - k) for s in range(64) for k in range(4)]


def exchange(block, stride):
    others = [lax.ppermute(block, "samp", [(i, i ^ stride * k) for i in range(64)]) for k in (1, 2, 3)]
    return [block] + others


def on_device(initial_state, target, control, point_index, generator):
    rows, width = initial_state.shape
    row_table = row_tables(rows * lax.axis_size("strip"))

    both = ("samp", "strip")
    own, to_core, to_z, wide_to_core, wide_to_z = strip_edges((initial_state, control, target))
    own = jnp.maximum(own, jnp.finfo(jnp.float32).min)
    core, far = lax.ppermute(to_core, both, CORES), lax.ppermute(to_z, both, ACROSS)
    core_wide, far_wide = lax.ppermute(wide_to_core, both, CORES), lax.ppermute(wide_to_z, both, ACROSS)
    points = jnp.broadcast_to(point_index[:, None, None], (SAMPLES, 1, 128))
    points = lax.all_to_all(points, "samp", 0, 0, tiled=True).reshape(SAMPLES, 128)
    mine = tile_gradient(points, generator.T, *tile_col_tables(width), row_table, core, own, far)

    tiles = jnp.stack(exchange(mine, 1))
    tiles, core_wide, far_wide = lax.optimization_barrier((tiles, core_wide, far_wide))
    tiles = jnp.stack(exchange(tiles, 16))
    tiles, generator = lax.optimization_barrier((tiles, generator))
    new_control = assemble(exchange(tiles, 4))

    state = own_final_state(point_index, generator, row_table, initial_state, control, core_wide, far_wide)
    return (new_control, state[None])


def solution(mesh):
    placed = (P("strip", None), P("strip", None), P("strip", None), P("samp"), P())
    return jax.shard_map(
        on_device,
        mesh=mesh,
        in_specs=placed,
        out_specs=(P("strip", None), P("samp", "strip", None)),
        check_vma=False,
    )
```
